256 devices in a mesh: dp: 8 (over x, z_hi), dap: 32 (over z_lo, y, core).
Axes of the slice: x: 4, y: 4, z: 8 (z_hi: 2, z_lo: 4; z = z_hi * 4 + z_lo), core: 2. Of those that a mesh axis runs over, the one named last changes fastest.
Arguments:
- pair_rep: bfloat16 [2048, 256, 128], P(('dp', 'dap')), parts along dimension 0, may hold values from -6 to 6
- cotangent: bfloat16 [2048, 256, 128], P(('dp', 'dap')), parts along dimension 0, may hold values from -6 to 6
- norm_gain: float32 [2, 128], replicated, may hold values from 0.5 to 1.5
- w_project: float32 [2, 128, 512], replicated, may hold values from -3 to 3
- w_bias: float32 [2, 128, 4], replicated, may hold values from -0.5 to 0.5
- w_out: float32 [2, 128, 128], replicated, may hold values from -0.5 to 0.5
Outputs:
- d_pair: bfloat16 [2048, 256, 128], P(('dp', 'dap')), parts along dimension 0
- grad_gain: float32 [16, 128], P('dp'), parts along dimension 0
- grad_project: float32 [16, 128, 512], P('dp'), parts along dimension 0
- grad_bias: float32 [16, 128, 4], P('dp'), parts along dimension 0
- grad_out: float32 [16, 128, 128], P('dp'), parts along dimension 0
The draws below stay inside these ranges and needn't reach their ends.
There are 8 independent parts, one for each index of `dp`. The reference program is written for one: setup_inputs(seed, part) draws one part's arguments, and reference() takes and returns one part's arrays. A program takes and returns all parts, laid end to end along the dimension named above; an argument that names none is the same for every part. Nothing has to cross between parts.
All inputs are finite; a program needn't handle non-finite values.
Results may differ from the reference program's by a relative error of at most 0.02.
The reference program's roundings to bfloat16 on the way count: a program that leaves them out, or rounds other values in their place, can miss the bound.
Values may be sent and summed in bfloat16 or wider, within the bound.
A program may use at most 64 MiB of HBM per device.

```python
import math
import jax
import jax.numpy as jnp
from jax import lax

C = 128
H = 4
N = 256


def draw_w_project(key, part):
    key = jax.random.fold_in(key, 7)
    first_key = jax.random.fold_in(key, 0)
    base = jnp.clip(jax.random.normal(first_key, (2, C, 4 * C), jnp.float32), -4.0, 4.0) / math.sqrt(C)
    return jnp.clip(base, -3.0, 3.0)


def shard_levels(stream_key, dims, cuts, low, largest):
    def one(dim, blocks):
        steps = jax.random.uniform(jax.random.fold_in(jax.random.fold_in(stream_key, 6), dim), (blocks,), jnp.float32, low / len(cuts), largest / len(cuts))
        return jnp.repeat(jnp.exp(steps), dims[dim] // blocks).reshape((-1,) + (1,) * (len(dims) - dim - 1))

    level = one(*cuts[0])
    for cut in cuts[1:]:
        level = level * one(*cut)
    return level


def normal_values(own_key, dims, width, bound, pieces=(), kind=jnp.bfloat16):
    values = jax.random.normal(own_key, dims, jnp.float32) * width
    if len(pieces) > 0:
        values = shard_levels(own_key, dims, pieces, -0.22, 0.18) * values
    return jnp.clip(values, min=-bound, max=bound).astype(kind)


def setup_inputs(seed: int = 0, part: int = 0) -> dict:
    streams_of = jax.random.split(jax.random.key(seed), 7)
    part_keys = jax.random.split(jax.random.fold_in(streams_of[6], part), 7)
    pair_rep = normal_values(part_keys[0], (N, N, C), 1.0, 6.0, ((0, 32),))
    cotangent = normal_values(part_keys[1], (N, N, C), 1.0, 6.0, ((0, 32),))
    norm_gain = jnp.clip(1.0 + 0.1 * jax.random.normal(streams_of[2], (2, C), jnp.float32), 0.5, 1.5)
    w_project = draw_w_project(jax.random.fold_in(streams_of[6], 71), part)
    w_bias = normal_values(streams_of[4], (2, C, H), C ** -0.5, 0.5, (), jnp.float32)
    w_out = normal_values(streams_of[5], (2, C, C), C ** -0.5, 0.5, (), jnp.float32)
    return dict(pair_rep=pair_rep, cotangent=cotangent, norm_gain=norm_gain, w_project=w_project, w_bias=w_bias, w_out=w_out)


EPS = 1e-05

def normalize(values_f, gain):
    row_mean = lax.optimization_barrier(jnp.mean(values_f, axis=-1, keepdims=True))
    centred = values_f - row_mean
    variance = lax.optimization_barrier(jnp.mean(centred * centred, axis=-1, keepdims=True))
    return centred * lax.rsqrt(variance + EPS) * gain

def project(pair_rows, gain, w_project, w_bias):
    normed = normalize(pair_rows.astype(jnp.float32), gain).astype(jnp.bfloat16)
    normed_f = normed.astype(jnp.float32)
    projected = jnp.einsum('rnc,cf->rnf', normed_f, w_project.astype(jnp.bfloat16).astype(jnp.float32))
    bias_rows = jnp.einsum('rnc,ch->hrn', normed_f, w_bias.astype(jnp.bfloat16).astype(jnp.float32)).astype(jnp.bfloat16)
    return (normed, projected, bias_rows)

def attend(projected, bias_all):
    channels = projected.shape[-1] // 4
    num_heads = bias_all.shape[0]
    head_size = channels // num_heads
    row_count, length = (projected.shape[0], projected.shape[1])
    shape_heads = (row_count, length, num_heads, head_size)
    queries = (projected[..., :channels] * head_size ** (-0.5)).astype(jnp.bfloat16).reshape(shape_heads)
    key_rows = projected[..., channels:2 * channels].astype(jnp.bfloat16).reshape(shape_heads)
    value_rows = projected[..., 2 * channels:3 * channels].astype(jnp.bfloat16).reshape(shape_heads)
    gate_vals = jax.nn.sigmoid(projected[..., 3 * channels:])
    scores = jnp.einsum('bqhd,bkhd->bhqk', queries.astype(jnp.float32), key_rows.astype(jnp.float32)) + bias_all[None]
    row_max = lax.optimization_barrier(jnp.max(scores, axis=-1, keepdims=True))
    exp_scores = jnp.exp(scores - row_max)
    soft_weights = (exp_scores / lax.optimization_barrier(jnp.sum(exp_scores, axis=-1, keepdims=True))).astype(jnp.bfloat16)
    mixture = jnp.einsum('bhqk,bkhd->bqhd', soft_weights.astype(jnp.float32), value_rows.astype(jnp.float32))
    return (mixture.reshape(row_count, length, channels) * gate_vals).astype(jnp.bfloat16)

def blocked(array):
    return array.reshape((array.shape[0] // 2, 2) + array.shape[1:])

def unblocked(array):
    return array.reshape((array.shape[0] * 2,) + array.shape[2:])

def layer_forward(pair_rows, gain, w_project, w_bias, w_out):
    normed, projected, bias_rows = project(pair_rows, gain, w_project, w_bias)
    bias_all = bias_rows.astype(jnp.float32)
    mixture = unblocked(lax.map(lambda one_block: attend(one_block, bias_all), blocked(projected)))
    out_term = jnp.einsum('rnc,cd->rnd', mixture.astype(jnp.float32), w_out.astype(jnp.bfloat16).astype(jnp.float32))
    return (pair_rows.astype(jnp.float32) + out_term).astype(jnp.bfloat16)

def layer_backward(pair_rows, grad_in, gain, w_project, w_bias, w_out):
    normed, projected, bias_rows = project(pair_rows, gain, w_project, w_bias)
    bias_all = bias_rows.astype(jnp.float32)
    grad_f = grad_in.astype(jnp.float32)
    w_out_f = w_out.astype(jnp.bfloat16).astype(jnp.float32)
    d_mixture = jnp.einsum('rnd,cd->rnc', grad_f, w_out_f).astype(jnp.bfloat16)

    def step(carry, inputs):
        proj_block, dmix_block = inputs
        mixture_block, pullback = jax.vjp(attend, proj_block, bias_all)
        d_proj_block, d_bias_block = pullback(dmix_block)
        return (carry + d_bias_block, (mixture_block, d_proj_block))
    d_bias_f, (mixture_b, d_proj_b) = lax.scan(step, jnp.zeros(bias_all.shape, jnp.float32), (blocked(projected), blocked(d_mixture)))
    mixture = unblocked(mixture_b)
    d_projected = unblocked(d_proj_b).astype(jnp.bfloat16).astype(jnp.float32)
    d_bias = d_bias_f.astype(jnp.bfloat16).astype(jnp.float32)
    normed_f = normed.astype(jnp.float32)
    grad_out = jnp.einsum('rnc,rnd->cd', mixture.astype(jnp.float32), grad_f)
    grad_project = jnp.einsum('rnc,rnf->cf', normed_f, d_projected)
    grad_bias = jnp.einsum('rnc,hrn->ch', normed_f, d_bias)
    d_normed = jnp.einsum('rnf,cf->rnc', d_projected, w_project.astype(jnp.bfloat16).astype(jnp.float32))
    d_normed = d_normed + jnp.einsum('hrn,ch->rnc', d_bias, w_bias.astype(jnp.bfloat16).astype(jnp.float32))
    unused, norm_pull = jax.vjp(normalize, pair_rows.astype(jnp.float32), gain)
    d_input, grad_gain = norm_pull(d_normed)
    d_rows = (grad_f + d_input).astype(jnp.bfloat16)
    return (d_rows, (grad_gain, grad_project, grad_bias, grad_out))

def reference(pair_rep, cotangent, norm_gain, w_project, w_bias, w_out):
    middle = layer_forward(pair_rep, norm_gain[0], w_project[0], w_bias[0], w_out[0])
    mid_cols = jnp.swapaxes(middle, 0, 1)
    cot_cols = jnp.swapaxes(cotangent, 0, 1)
    d_mid_cols, grads_two = layer_backward(mid_cols, cot_cols, norm_gain[1], w_project[1], w_bias[1], w_out[1])
    d_middle = jnp.swapaxes(d_mid_cols, 0, 1)
    d_pair, grads_one = layer_backward(pair_rep, d_middle, norm_gain[0], w_project[0], w_bias[0], w_out[0])
    return (d_pair, jnp.stack([grads_one[0], grads_two[0]]), jnp.stack([grads_one[1], grads_two[1]]), jnp.stack([grads_one[2], grads_two[2]]), jnp.stack([grads_one[3], grads_two[3]]))
```

```python
import jax
import jax.numpy as jnp
from jax import lax
from jax.experimental import pallas as pl
from jax.experimental.pallas import tpu as pltpu
from jax.sharding import PartitionSpec as P

EPS = 1e-05
MESH = pl.DeviceIdType.MESH
DAP = 32


def peer_of(me, step):
    return lax.rem(me + step, DAP)


def greet(me):
    barrier = pltpu.get_barrier_semaphore()

    def tell(step, carry):
        pl.semaphore_signal(
            barrier, inc=1, device_id=(lax.axis_index("dp"), peer_of(me, step)), device_id_type=MESH
        )
        return carry

    lax.fori_loop(1, DAP, tell, 0)
    pl.semaphore_wait(barrier, DAP - 1)


def send(src, dst, send_sem, recv_sem, peer):
    return pltpu.make_async_remote_copy(
        src_ref=src,
        dst_ref=dst,
        send_sem=send_sem,
        recv_sem=recv_sem,
        device_id=(lax.axis_index("dp"), peer),
        device_id_type=MESH,
    )


def exchange(me, source, into, send_sem, recv_sem):
    def start(step, carry):
        peer = peer_of(me, step)
        send(source(peer), into(me), send_sem.at[peer], recv_sem.at[me], peer).start()
        return carry

    def finish(step, carry):
        peer = peer_of(me, DAP - step)
        send(source(peer), into(peer), send_sem.at[peer], recv_sem.at[peer], peer).wait()
        return carry

    lax.fori_loop(1, DAP, start, 0)
    lax.fori_loop(1, DAP, finish, 0)


def gather_kernel(x_ref, out_ref, send_sem, recv_sem):
    me = lax.axis_index("dap")
    greet(me)
    out_ref[me] = x_ref[...]
    exchange(me, lambda peer: x_ref, lambda slot: out_ref.at[slot], send_sem, recv_sem)


def swap_kernel(x_ref, out_ref, send_sem, recv_sem):
    me = lax.axis_index("dap")
    greet(me)
    out_ref[me] = x_ref[me]
    exchange(me, lambda peer: x_ref.at[peer], lambda slot: out_ref.at[slot], send_sem, recv_sem)


def scatter_sum_kernel(x_ref, out_ref, held, send_sem, recv_sem):
    me = lax.axis_index("dap")
    greet(me)
    held[me] = x_ref[me]
    exchange(me, lambda peer: x_ref.at[peer], lambda slot: held.at[slot], send_sem, recv_sem)
    out_ref[...] = lax.fori_loop(
        0, DAP, lambda slot, total: total + held[slot], jnp.zeros(out_ref.shape, jnp.float32)
    )


def sum_kernel(x_ref, out_ref, held, mine, send_sem, recv_sem, send_two, recv_two):
    me = lax.axis_index("dap")
    greet(me)
    held[me] = x_ref[me]
    exchange(me, lambda peer: x_ref.at[peer], lambda slot: held.at[slot], send_sem, recv_sem)
    total = lax.fori_loop(
        0, DAP, lambda slot, total: total + held[slot], jnp.zeros(mine.shape, jnp.float32)
    )
    mine[...] = total
    out_ref[me] = total
    exchange(me, lambda peer: mine, lambda slot: out_ref.at[slot], send_two, recv_two)


def call(kernel, number, out, scratch, *arrays):
    return pl.pallas_call(
        kernel,
        out_shape=out,
        in_specs=[pl.BlockSpec(memory_space=pltpu.VMEM)] * len(arrays),
        out_specs=pl.BlockSpec(memory_space=pltpu.VMEM),
        scratch_shapes=scratch,
        compiler_params=pltpu.CompilerParams(
            collective_id=number, has_side_effects=True, vmem_limit_bytes=32 << 20
        ),
    )(*arrays)


def sems(count):
    return [pltpu.SemaphoreType.DMA((DAP,))] * count


def gather(x, number):
    return call(gather_kernel, number, jax.ShapeDtypeStruct((DAP,) + x.shape, x.dtype), sems(2), x)


def swap(x, number):
    return call(swap_kernel, number, jax.ShapeDtypeStruct(x.shape, x.dtype), sems(2), x)


def scatter_sum(x, number):
    return call(
        scatter_sum_kernel,
        number,
        jax.ShapeDtypeStruct(x.shape[1:], x.dtype),
        [pltpu.VMEM(x.shape, x.dtype)] + sems(2),
        x,
    )


def sum_all(x, number):
    return call(
        sum_kernel,
        number,
        jax.ShapeDtypeStruct(x.shape, x.dtype),
        [pltpu.VMEM(x.shape, x.dtype), pltpu.VMEM(x.shape[1:], x.dtype)] + sems(4),
        x,
    )


def normalize(values_f, gain):
    row_mean = jnp.mean(values_f, axis=-1, keepdims=True)
    centred = values_f - row_mean
    variance = jnp.mean(centred * centred, axis=-1, keepdims=True)
    return centred * lax.rsqrt(variance + EPS) * gain


def project(pair_rows, gain, w_project, w_bias):
    normed = normalize(pair_rows.astype(jnp.float32), gain).astype(jnp.bfloat16)
    projected = jnp.einsum(
        "rnc,cf->rnf", normed, w_project.astype(jnp.bfloat16), preferred_element_type=jnp.float32
    )
    bias_rows = jnp.einsum(
        "rnc,ch->hrn", normed, w_bias.astype(jnp.bfloat16), preferred_element_type=jnp.float32
    ).astype(jnp.bfloat16)
    return (normed, projected, bias_rows)


def attend(projected, bias_all):
    channels = projected.shape[-1] // 4
    num_heads = bias_all.shape[0]
    head_size = channels // num_heads
    row_count, length = (projected.shape[0], projected.shape[1])
    shape_heads = (row_count, length, num_heads, head_size)
    queries = (
        (projected[..., :channels] * head_size ** (-0.5)).astype(jnp.bfloat16).reshape(shape_heads)
    )
    key_rows = projected[..., channels : 2 * channels].astype(jnp.bfloat16).reshape(shape_heads)
    value_rows = (
        projected[..., 2 * channels : 3 * channels].astype(jnp.bfloat16).reshape(shape_heads)
    )
    gate_vals = jax.nn.sigmoid(projected[..., 3 * channels :])
    scores = (
        jnp.einsum("bqhd,bkhd->bhqk", queries, key_rows, preferred_element_type=jnp.float32)
        + bias_all[None]
    )
    row_max = jnp.max(scores, axis=-1, keepdims=True)
    exp_scores = jnp.exp(scores - row_max)
    soft_weights = (exp_scores / jnp.sum(exp_scores, axis=-1, keepdims=True)).astype(jnp.bfloat16)
    mixture = jnp.einsum(
        "bhqk,bkhd->bqhd", soft_weights, value_rows, preferred_element_type=jnp.float32
    )
    return (mixture.reshape(row_count, length, channels) * gate_vals).astype(jnp.bfloat16)


def blocked(array):
    return array.reshape((array.shape[0] // 2, 2) + array.shape[1:])


def unblocked(array):
    return array.reshape((array.shape[0] * 2,) + array.shape[2:])


def gather_bias(bias_rows, number):
    heads, rows, length = bias_rows.shape
    parts = gather(bias_rows.reshape(heads * rows, length), number)
    parts = parts.reshape(DAP, heads, rows, length).swapaxes(0, 1)
    return parts.reshape(heads, DAP * rows, length).astype(jnp.float32)


def to_columns(piece, number):
    rows, length, channels = piece.shape
    sent = piece.reshape(rows, DAP, rows, channels).transpose(1, 0, 2, 3)
    got = swap(sent.reshape(DAP, rows * rows, channels), number)
    got = got.reshape(DAP, rows, rows, channels).transpose(2, 0, 1, 3)
    return got.reshape(rows, length, channels)


def scatter_bias(d_bias_part, number):
    heads, length, _ = d_bias_part.shape
    rows = length // DAP
    sent = d_bias_part.reshape(heads, DAP, rows, length).swapaxes(0, 1)
    got = scatter_sum(sent.reshape(DAP, heads * rows, length), number)
    return got.reshape(heads, rows, length).astype(jnp.bfloat16)


def sum_grads(grads, number):
    flat = jnp.concatenate([grad.reshape(-1) for grad in grads])
    step = DAP * 8 * 128
    size = -(-flat.shape[0] // step) * step
    padded = jnp.pad(flat, (0, size - flat.shape[0])).reshape(DAP, size // DAP // 128, 128)
    total = sum_all(padded, number).reshape(-1)
    out, at = [], 0
    for grad in grads:
        out.append(total[at : at + grad.size].reshape(grad.shape))
        at += grad.size
    return tuple(out)


def layer_backward(pair_rows, grad_in, normed, projected, bias_all, gain, w_project, w_bias, w_out, number):
    grad_f = grad_in.astype(jnp.float32)
    d_mixture = jnp.einsum(
        "rnd,cd->rnc", grad_in, w_out.astype(jnp.bfloat16), preferred_element_type=jnp.float32
    ).astype(jnp.bfloat16)

    def step(carry, inputs):
        proj_block, dmix_block = inputs
        mixture_block, pullback = jax.vjp(attend, proj_block, bias_all)
        d_proj_block, d_bias_block = pullback(dmix_block)
        return (carry + d_bias_block, (mixture_block, d_proj_block))

    d_bias_part, (mixture_b, d_proj_b) = lax.scan(
        step, jnp.zeros(bias_all.shape, jnp.float32), (blocked(projected), blocked(d_mixture))
    )
    mixture = unblocked(mixture_b)
    d_projected = unblocked(d_proj_b).astype(jnp.bfloat16)
    d_bias = scatter_bias(d_bias_part, number)
    grad_out = jnp.einsum("rnc,rnd->cd", mixture, grad_in, preferred_element_type=jnp.float32)
    grad_project = jnp.einsum(
        "rnc,rnf->cf", normed, d_projected, preferred_element_type=jnp.float32
    )
    grad_bias = jnp.einsum("rnc,hrn->ch", normed, d_bias, preferred_element_type=jnp.float32)
    d_normed = jnp.einsum(
        "rnf,cf->rnc",
        d_projected,
        w_project.astype(jnp.bfloat16),
        preferred_element_type=jnp.float32,
    )
    d_normed = d_normed + jnp.einsum(
        "hrn,ch->rnc", d_bias, w_bias.astype(jnp.bfloat16), preferred_element_type=jnp.float32
    )
    unused, norm_pull = jax.vjp(normalize, pair_rows.astype(jnp.float32), gain)
    d_input, grad_gain = norm_pull(d_normed)
    d_rows = (grad_f + d_input).astype(jnp.bfloat16)
    return (d_rows, (grad_gain, grad_project, grad_bias, grad_out))


def per_device(pair_rep, cotangent, norm_gain, w_project, w_bias, w_out):
    normed_one, proj_one, bias_one = project(pair_rep, norm_gain[0], w_project[0], w_bias[0])
    bias_all_one = gather_bias(bias_one, 0)
    mixture_one = unblocked(
        lax.map(lambda one_block: attend(one_block, bias_all_one), blocked(proj_one))
    )
    out_one = jnp.einsum(
        "rnc,cd->rnd",
        mixture_one,
        w_out[0].astype(jnp.bfloat16),
        preferred_element_type=jnp.float32,
    )
    middle = (pair_rep.astype(jnp.float32) + out_one).astype(jnp.bfloat16)
    mid_cols, cot_cols = (to_columns(middle, 2), to_columns(cotangent, 3))
    normed_two, proj_two, bias_two = project(mid_cols, norm_gain[1], w_project[1], w_bias[1])
    bias_all_two = gather_bias(bias_two, 1)
    d_mid_cols, grads_two = layer_backward(
        mid_cols,
        cot_cols,
        normed_two,
        proj_two,
        bias_all_two,
        norm_gain[1],
        w_project[1],
        w_bias[1],
        w_out[1],
        5,
    )
    d_middle = to_columns(d_mid_cols, 4)
    d_pair, grads_one = layer_backward(
        pair_rep,
        d_middle,
        normed_one,
        proj_one,
        bias_all_one,
        norm_gain[0],
        w_project[0],
        w_bias[0],
        w_out[0],
        6,
    )
    stacked = tuple(
        (
            jnp.stack([first_grad, second_grad])
            for first_grad, second_grad in zip(grads_one, grads_two)
        )
    )
    stacked = sum_grads(stacked, 7)
    return (d_pair, stacked[0], stacked[1], stacked[2], stacked[3])


def solution(mesh):
    in_specs = (P(("dp", "dap"), None, None), P(("dp", "dap"), None, None), P(), P(), P(), P())
    out_specs = (
        P(("dp", "dap"), None, None),
        P("dp", None),
        P("dp", None, None),
        P("dp", None, None),
        P("dp", None, None),
    )
    return jax.shard_map(
        per_device, mesh=mesh, in_specs=in_specs, out_specs=out_specs, check_vma=False
    )
```

```python
import jax
import jax.numpy as jnp
from jax import lax
from jax.experimental import pallas as pl
from jax.experimental.pallas import tpu as pltpu
from jax.sharding import PartitionSpec as P

EPS = 1e-05
MESH = pl.DeviceIdType.MESH
F32 = jnp.float32
BF16 = jnp.bfloat16
DAP = 32
ROWS = 8
LENGTH = 256
CHANNELS = 128
HEADS = 4
BLOCKS = 4
BLOCK = LENGTH // BLOCKS
STACK = HEADS * BLOCK
SCALE = (CHANNELS // HEADS) ** (-0.5)


def slot_of(device):
    return (
        lax.rem(lax.div(device, 2), 4) * 8 + lax.div(device, 8) * 2 + lax.rem(device, 2)
    )


def device_of(slot):
    return lax.rem(lax.div(slot, 2), 4) * 8 + lax.div(slot, 8) * 2 + lax.rem(slot, 2)


def remote(src, dst, send_sem, recv_sem, slot):
    return pltpu.make_async_remote_copy(
        src_ref=src,
        dst_ref=dst,
        send_sem=send_sem,
        recv_sem=recv_sem,
        device_id=(lax.axis_index("dp"), device_of(slot)),
        device_id_type=MESH,
    )


def loop(low, high, body):
    def step(index, carry):
        body(index)
        return carry

    lax.fori_loop(low, high, step, 0)


def dot(a, b):
    return lax.dot_general(a, b, (((1,), (0,)), ((), ())), preferred_element_type=F32)


def dot_nt(a, b):
    return lax.dot_general(a, b, (((1,), (1,)), ((), ())), preferred_element_type=F32)


def dot_tn(a, b):
    return lax.dot_general(a, b, (((0,), (0,)), ((), ())), preferred_element_type=F32)


def centre(values):
    centred = values - jnp.mean(values, axis=-1, keepdims=True)
    variance = jnp.mean(centred * centred, axis=-1, keepdims=True)
    inverse = lax.rsqrt(variance + EPS)
    return centred * inverse, inverse


def kernel(
    x_ref,
    cot_ref,
    gain_ref,
    wp_ref,
    wb_ref,
    wo_ref,
    dpair_ref,
    small_ref,
    gproj_ref,
    gout_ref,
    rows_s,
    dy_s,
    norm_s,
    q_s,
    k_s,
    v_s,
    gate_s,
    o_s,
    mix_s,
    p_s,
    dproj_s,
    dkt_s,
    dvt_s,
    wp_s,
    wo_s,
    bias_f,
    bias_all,
    bias_q,
    dm_s,
    dbias_acc,
    wide_s,
    stage_s,
    cot_send,
    cot_recv,
    mid_send,
    mid_recv,
    back_send,
    back_recv,
    db_kept,
    db_pair_send,
    db_pair_recv,
    db_send,
    db_recv,
    db_s,
    wg_send,
    wg_recv,
    wg_all,
    sg_all,
    cot_ss,
    cot_rs,
    mid_ss,
    mid_rs,
    back_ss,
    back_rs,
    bias_ss,
    bias_fs,
    bias_rs,
    pair_ss,
    pair_rs,
    db_ss,
    db_rs,
    wg_ss,
    wg_rs,
    wa_ss,
    wa_fs,
    wa_rs,
    sg_ss,
    sg_rs,
):
    me = slot_of(lax.axis_index("dap"))
    mine = lax.div(me, 2)
    core = lax.rem(me, 2)
    sibling = me + 1 - 2 * core
    first_block = lax.div(me, 8)
    barrier = pltpu.get_barrier_semaphore()

    def other(step):
        return lax.rem(me + step, DAP)

    def tell(step):
        pl.semaphore_signal(
            barrier,
            inc=1,
            device_id=(lax.axis_index("dp"), device_of(other(step))),
            device_id_type=MESH,
        )

    loop(1, DAP, tell)

    lane_head = lax.div(lax.broadcasted_iota(jnp.int32, (1, CHANNELS), 1), CHANNELS // HEADS)
    masks = [jnp.where(lane_head == head, 1.0, 0.0).astype(F32) for head in range(HEADS)]
    masks_short = [mask.astype(BF16) for mask in masks]

    def stack(block):
        return jnp.concatenate([block * mask for mask in masks_short], axis=0)

    def pick(stacked):
        out = stacked[:BLOCK] * masks[0]
        for head in range(1, HEADS):
            out = out + stacked[head * BLOCK : (head + 1) * BLOCK] * masks[head]
        return out

    def block_rows(block):
        return pl.ds(pl.multiple_of(block * BLOCK, BLOCK), BLOCK)

    def gather_start(buf, ss, rs):
        remote(buf.at[me], buf.at[me], ss.at[sibling], rs.at[me], sibling).start()

        def go(step):
            slot = other(2 * step)
            remote(buf.at[me], buf.at[me], ss.at[slot], rs.at[me], slot).start()

        loop(1, DAP // 2, go)

    def gather_finish(buf, ss, fs, rs):
        def forward(step):
            slot = other(DAP - 2 * step)
            remote(buf.at[slot], buf.at[slot], ss.at[slot], rs.at[slot], slot).wait_recv()
            remote(buf.at[slot], buf.at[slot], fs.at[slot], rs.at[slot], sibling).start()

        loop(1, DAP // 2, forward)

        def take(chip):
            slot = 2 * chip + 1 - core
            remote(buf.at[slot], buf.at[slot], ss.at[slot], rs.at[slot], slot).wait_recv()

        loop(0, DAP // 2, take)

    def gather_sent(buf, ss, fs, rs):
        remote(buf.at[me], buf.at[me], ss.at[sibling], rs.at[me], sibling).wait_send()

        def done(step):
            slot = other(2 * step)
            remote(buf.at[me], buf.at[me], ss.at[slot], rs.at[me], slot).wait_send()
            remote(buf.at[slot], buf.at[slot], fs.at[slot], rs.at[slot], sibling).wait_send()

        loop(1, DAP // 2, done)

    def swap_start(send, recv, ss, rs, slot):
        @pl.when(slot != me)
        def _():
            remote(send.at[slot], recv.at[me], ss.at[slot], rs.at[me], slot).start()

    def swap_take(send, recv, ss, rs, slot):
        @pl.when(slot != me)
        def _():
            remote(send.at[slot], recv.at[slot], ss.at[slot], rs.at[slot], slot).wait_recv()

    def swap_sent(send, recv, ss, rs):
        def done(step):
            slot = other(step)
            remote(send.at[slot], recv.at[me], ss.at[slot], rs.at[me], slot).wait_send()

        loop(1, DAP, done)

    def normalise(layer, take_row):
        def row(index):
            values = take_row(index)
            hat, _ = centre(values)
            normed = (hat * gain_ref[layer : layer + 1, :]).astype(BF16)
            norm_s[layer, index] = normed
            bias = dot_nt(wb_ref[layer].astype(BF16), normed)
            for half in range(2):
                bias_f[half, pl.ds(index, HEADS, stride=ROWS), :] = bias[
                    :HEADS, half * CHANNELS : (half + 1) * CHANNELS
                ]

        loop(0, ROWS, row)
        bias_all[layer, me] = jnp.concatenate([bias_f[0], bias_f[1]], axis=1).astype(BF16)

    def project(layer):
        def row(index):
            projected = dot(norm_s[layer, index], wp_s[layer])
            q_s[layer, index] = (projected[:, :CHANNELS] * SCALE).astype(BF16)
            k_s[layer, index] = projected[:, CHANNELS : 2 * CHANNELS].astype(BF16)
            v_s[layer, index] = projected[:, 2 * CHANNELS : 3 * CHANNELS].astype(BF16)
            gate_s[layer, index] = 1.0 / (1.0 + jnp.exp(-projected[:, 3 * CHANNELS :]))

        loop(0, ROWS, row)

    def spread_bias(layer, block):
        for part in range(8):
            piece = bias_all[layer, block * 8 + part].astype(F32)
            for head in range(HEADS):
                at = head * BLOCK + part * ROWS
                bias_q[at : at + ROWS, :] = piece[head * ROWS : (head + 1) * ROWS]

    def weights(layer, index, block):
        queries = stack(q_s[layer, index, block_rows(block), :])
        scores = dot_nt(queries, k_s[layer, index]) + bias_q[...]
        shifted = jnp.exp(scores - jnp.max(scores, axis=-1, keepdims=True))
        return queries, shifted * (1.0 / jnp.sum(shifted, axis=-1, keepdims=True))

    def mix(layer, index, block, short):
        mixed = pick(dot(short, v_s[layer, index]))
        o_s[layer, index, block_rows(block), :] = mixed
        gate = gate_s[layer, index, block_rows(block), :]
        mix_s[layer, index, block_rows(block), :] = (mixed * gate).astype(BF16)
        return mixed

    def backward(layer, load_dy):
        dkt_s[...] = jnp.zeros(dkt_s.shape, F32)
        dvt_s[...] = jnp.zeros(dvt_s.shape, F32)

        def pass_on(block):
            remote(
                db_pair_send.at[layer, block],
                db_pair_recv.at[layer, block],
                pair_ss.at[layer, block],
                pair_rs.at[layer, block],
                sibling,
            ).wait_recv()
            for z in range(4):
                total = db_kept[block, z] + db_pair_recv[layer, block, z].astype(F32)
                db_send[layer, block, z] = total.astype(BF16)
                slot = block * 8 + z * 2 + core

                @pl.when(slot != me)
                def _():
                    remote(
                        db_send.at[layer, block, z],
                        db_recv.at[layer, mine],
                        db_ss.at[layer, block * 4 + z],
                        db_rs.at[layer, mine],
                        slot,
                    ).start()

                @pl.when(slot == me)
                def _():
                    db_recv[layer, mine] = db_send[layer, block, z]

        def step_block(step):
            block = lax.rem(first_block + step, BLOCKS)
            load_dy(block)
            dy = dy_s[layer, :, block_rows(block), :].reshape(ROWS * BLOCK, CHANNELS)
            dm_s[...] = dot_nt(dy, wo_s[layer]).astype(BF16).astype(F32).reshape(dm_s.shape)
            spread_bias(layer, block)
            dbias_acc[...] = jnp.zeros(dbias_acc.shape, F32)

            def row(index):
                at = block_rows(block)
                if layer == 0:
                    queries = stack(q_s[layer, index, at, :])
                    short = p_s[index, block]
                    soft = short.astype(F32)
                    mixed = o_s[layer, index, at, :]
                else:
                    queries, soft = weights(layer, index, block)
                    short = soft.astype(BF16)
                    mixed = mix(layer, index, block, short)
                gate = gate_s[layer, index, at, :]
                dm = dm_s[index]
                d_gate = dm * mixed * gate * (1.0 - gate)
                dproj_s[index, at, 3 * CHANNELS :] = d_gate.astype(BF16)
                d_mixed = stack((dm * gate).astype(BF16))
                d_soft = dot_nt(d_mixed, v_s[layer, index]).astype(BF16).astype(F32)
                product = soft * d_soft
                d_scores = product - soft * jnp.sum(product, axis=-1, keepdims=True)
                dbias_acc[...] += d_scores
                d_short = d_scores.astype(BF16)
                d_query = pick(dot(d_short, k_s[layer, index])).astype(BF16).astype(F32)
                dproj_s[index, at, :CHANNELS] = (d_query * SCALE).astype(BF16)
                dkt_s[index] += dot_tn(queries, d_short)
                dvt_s[index] += dot_tn(d_mixed, short)

            loop(0, ROWS, row)
            for z in range(4):
                for half in range(2):
                    part = z * 2 + half
                    piece = jnp.concatenate(
                        [
                            dbias_acc[
                                head * BLOCK + part * ROWS : head * BLOCK + (part + 1) * ROWS, :
                            ]
                            for head in range(HEADS)
                        ],
                        axis=0,
                    )

                    @pl.when(core == half)
                    def _():
                        db_kept[block, z] = piece

                    @pl.when(core != half)
                    def _():
                        db_pair_send[layer, block, z] = piece.astype(BF16)

            remote(
                db_pair_send.at[layer, block],
                db_pair_recv.at[layer, block],
                pair_ss.at[layer, block],
                pair_rs.at[layer, block],
                sibling,
            ).start()

            @pl.when(step > 0)
            def _():
                pass_on(lax.rem(first_block + step + BLOCKS - 1, BLOCKS))

        loop(0, BLOCKS, step_block)
        pass_on(lax.rem(first_block + BLOCKS - 1, BLOCKS))

        wide_s[...] = jnp.zeros(wide_s.shape, F32)

        def row_grads(index):
            dproj_s[index, :, CHANNELS : 2 * CHANNELS] = dkt_s[index].T.astype(BF16)
            dproj_s[index, :, 2 * CHANNELS : 3 * CHANNELS] = dvt_s[index].T.astype(BF16)
            wide_s[:, : 4 * CHANNELS] += dot_tn(norm_s[layer, index], dproj_s[index])
            wide_s[:, 4 * CHANNELS :] += dot_tn(mix_s[layer, index], dy_s[layer, index])

        loop(0, ROWS, row_grads)

        def share(slot):
            at = pl.ds(pl.multiple_of(lax.div(slot, 2) * 8, 8), 8)
            half = lax.rem(slot, 2)

            @pl.when(half == 0)
            def _():
                wg_send[layer, slot, :, : 2 * CHANNELS] = wide_s[at, : 2 * CHANNELS]

            @pl.when(half == 1)
            def _():
                wg_send[layer, slot, :, : 2 * CHANNELS] = wide_s[at, 2 * CHANNELS : 4 * CHANNELS]

            wg_send[layer, slot, :, 2 * CHANNELS :] = wide_s[at, 4 * CHANNELS :]

        loop(0, DAP, share)
        loop(
            1,
            DAP,
            lambda step: swap_start(
                wg_send.at[layer], wg_recv.at[layer], wg_ss.at[layer], wg_rs.at[layer], other(step)
            ),
        )
        wg_recv[layer, me] = wg_send[layer, me]

    def finish_bias(layer):
        def take(chip):
            @pl.when(chip != mine)
            def _():
                remote(
                    db_send.at[layer, 0, 0],
                    db_recv.at[layer, chip],
                    db_ss.at[layer, chip],
                    db_rs.at[layer, chip],
                    sibling,
                ).wait_recv()

        loop(0, DAP // 2, take)
        total = lax.fori_loop(
            0,
            DAP // 2,
            lambda chip, total: total + db_recv[layer, chip].astype(F32),
            jnp.zeros((HEADS * ROWS, LENGTH), F32),
        )
        for half in range(2):
            db_s[half] = (
                total[:, half * CHANNELS : (half + 1) * CHANNELS].astype(BF16).astype(F32)
            )

    def input_grads(layer, emit):
        finish_bias(layer)
        zero = jnp.zeros((ROWS, CHANNELS), F32)
        weight = wb_ref[layer].astype(BF16)
        gain = gain_ref[layer : layer + 1, :]

        def head_rows(index):
            at = pl.ds(index, HEADS, stride=ROWS)
            rows = jnp.concatenate([db_s[0, at, :], db_s[1, at, :]], axis=1)
            return jnp.concatenate([rows, jnp.zeros((ROWS - HEADS, LENGTH), F32)], axis=0)

        grad_bias = lax.fori_loop(
            0,
            ROWS,
            lambda index, total: total
            + dot(head_rows(index).astype(BF16), norm_s[layer, index]),
            zero,
        )

        def row(index, total):
            d_normed = dot_nt(dproj_s[index], wp_s[layer]) + dot_tn(
                head_rows(index).astype(BF16), weight
            )
            hat, inverse = centre(rows_s[layer, index].astype(F32))
            d_hat = d_normed * gain
            d_input = inverse * (
                d_hat
                - jnp.mean(d_hat, axis=-1, keepdims=True)
                - hat * jnp.mean(d_hat * hat, axis=-1, keepdims=True)
            )
            emit(index, dy_s[layer, index].astype(F32) + d_input)
            return total + jnp.sum(d_normed * hat, axis=0, keepdims=True)

        grad_gain = lax.fori_loop(0, ROWS, row, jnp.zeros((1, CHANNELS), F32))
        sg_all[layer, me] = jnp.concatenate(
            [grad_bias[:HEADS], grad_gain, zero[: ROWS - HEADS - 1]], axis=0
        )

        def go(step):
            slot = other(step)
            remote(
                sg_all.at[layer, me],
                sg_all.at[layer, me],
                sg_ss.at[layer, slot],
                sg_rs.at[layer, me],
                slot,
            ).start()

        loop(1, DAP, go)

    def weight_sums(layer):
        loop(
            1,
            DAP,
            lambda step: swap_take(
                wg_send.at[layer],
                wg_recv.at[layer],
                wg_ss.at[layer],
                wg_rs.at[layer],
                other(DAP - step),
            ),
        )
        wg_all[layer, me] = lax.fori_loop(
            0,
            DAP,
            lambda slot, total: total + wg_recv[layer, slot],
            jnp.zeros((ROWS, 3 * CHANNELS), F32),
        )
        gather_start(wg_all.at[layer], wa_ss.at[layer], wa_rs.at[layer])

    def weight_out(layer):
        gather_finish(wg_all.at[layer], wa_ss.at[layer], wa_fs.at[layer], wa_rs.at[layer])

        def place(chip):
            at = pl.ds(pl.multiple_of(chip * 8, 8), 8)
            gproj_ref[layer, at, : 2 * CHANNELS] = wg_all[layer, 2 * chip, :, : 2 * CHANNELS]
            gproj_ref[layer, at, 2 * CHANNELS :] = wg_all[layer, 2 * chip + 1, :, : 2 * CHANNELS]
            gout_ref[layer, at, :] = wg_all[layer, 2 * chip, :, 2 * CHANNELS :]

        loop(0, DAP // 2, place)

        def take(step):
            slot = other(DAP - step)
            remote(
                sg_all.at[layer, slot],
                sg_all.at[layer, slot],
                sg_ss.at[layer, slot],
                sg_rs.at[layer, slot],
                slot,
            ).wait_recv()

        loop(1, DAP, take)
        small_ref[layer] = lax.fori_loop(
            0,
            DAP,
            lambda slot, total: total + sg_all[layer, slot],
            jnp.zeros((ROWS, CHANNELS), F32),
        )

    for layer in range(2):
        wp_s[layer] = wp_ref[layer].astype(BF16)
        wo_s[layer] = wo_ref[layer].astype(BF16)
    for y in range(4):
        for z in range(4):
            rows_s[0, :, y * 64 + z * 16 : y * 64 + z * 16 + 16, :] = x_ref[
                :, z * 64 + y * 16 : z * 64 + y * 16 + 16, :
            ]
    normalise(0, lambda index: rows_s[0, index].astype(F32))
    pl.semaphore_wait(barrier, DAP - 1)
    gather_start(bias_all.at[0], bias_ss.at[0], bias_rs.at[0])

    stage_s[...] = cot_ref[...].astype(F32).reshape(stage_s.shape)

    def stage_cot(slot):
        at = device_of(slot) * ROWS
        cot_send[slot] = jnp.concatenate(
            [
                stage_s[pl.ds(pl.multiple_of(row * LENGTH + at, ROWS), ROWS), :]
                for row in range(ROWS)
            ],
            axis=0,
        ).astype(BF16)

    loop(0, DAP, stage_cot)
    loop(1, DAP, lambda step: swap_start(cot_send, cot_recv, cot_ss, cot_rs, other(step)))
    cot_recv[me] = cot_send[me]
    project(0)
    gather_finish(bias_all.at[0], bias_ss.at[0], bias_fs.at[0], bias_rs.at[0])

    def forward_block(step):
        block = lax.rem(first_block + step, BLOCKS)
        spread_bias(0, block)

        def row(index):
            _, soft = weights(0, index, block)
            short = soft.astype(BF16)
            p_s[index, block] = short
            mix(0, index, block, short)

        loop(0, ROWS, row)
        mixture = mix_s[0, :, block_rows(block), :].reshape(ROWS * BLOCK, CHANNELS)
        term = dot(mixture, wo_s[0]).reshape(ROWS, BLOCK, CHANNELS)
        middle = rows_s[0, :, block_rows(block), :].astype(F32) + term
        for part in range(8):
            slot = block * 8 + part
            mid_send[slot] = (
                middle[:, part * ROWS : (part + 1) * ROWS, :]
                .reshape(ROWS * ROWS, CHANNELS)
                .astype(BF16)
            )
            swap_start(mid_send, mid_recv, mid_ss, mid_rs, slot)

    loop(0, BLOCKS, forward_block)
    mid_recv[me] = mid_send[me]

    loop(1, DAP, lambda step: swap_take(mid_send, mid_recv, mid_ss, mid_rs, other(DAP - step)))
    stage_s[...] = mid_recv[...].astype(F32).reshape(stage_s.shape)

    def middle_row(index):
        values = stage_s[pl.ds(index, LENGTH, stride=ROWS), :]
        rows_s[1, index] = values.astype(BF16)
        return values

    normalise(1, middle_row)
    gather_start(bias_all.at[1], bias_ss.at[1], bias_rs.at[1])
    loop(1, DAP, lambda step: swap_take(cot_send, cot_recv, cot_ss, cot_rs, other(DAP - step)))
    stage_s[...] = cot_recv[...].astype(F32).reshape(stage_s.shape)

    def cot_row(index):
        dy_s[1, index] = stage_s[pl.ds(index, LENGTH, stride=ROWS), :].astype(BF16)

    loop(0, ROWS, cot_row)
    project(1)
    gather_finish(bias_all.at[1], bias_ss.at[1], bias_fs.at[1], bias_rs.at[1])
    backward(1, lambda block: None)

    def emit_back(index, values):
        stage_s[pl.ds(index, LENGTH, stride=ROWS), :] = values

    input_grads(1, emit_back)
    back_send[...] = stage_s[...].astype(BF16).reshape(back_send.shape)
    loop(1, DAP, lambda step: swap_start(back_send, back_recv, back_ss, back_rs, other(step)))
    back_recv[me] = back_send[me]

    def load_back(block):
        for part in range(8):
            swap_take(back_send, back_recv, back_ss, back_rs, block * 8 + part)
        pieces = [
            back_recv[block * 8 + part].astype(F32).reshape(ROWS, ROWS, CHANNELS)
            for part in range(8)
        ]
        dy_s[0, :, block_rows(block), :] = jnp.concatenate(pieces, axis=1).astype(BF16)

    backward(0, load_back)
    weight_sums(1)

    def emit_pair(index, values):
        short = values.astype(BF16)
        for y in range(4):
            for z in range(4):
                dpair_ref[index, z * 64 + y * 16 : z * 64 + y * 16 + 16, :] = short[
                    y * 64 + z * 16 : y * 64 + z * 16 + 16
                ]

    input_grads(0, emit_pair)
    weight_sums(0)
    weight_out(1)
    weight_out(0)

    swap_sent(cot_send, cot_recv, cot_ss, cot_rs)
    swap_sent(mid_send, mid_recv, mid_ss, mid_rs)
    swap_sent(back_send, back_recv, back_ss, back_rs)
    for layer in range(2):
        gather_sent(bias_all.at[layer], bias_ss.at[layer], bias_fs.at[layer], bias_rs.at[layer])
        gather_sent(wg_all.at[layer], wa_ss.at[layer], wa_fs.at[layer], wa_rs.at[layer])
        swap_sent(wg_send.at[layer], wg_recv.at[layer], wg_ss.at[layer], wg_rs.at[layer])

        def small_sent(step):
            slot = other(step)
            remote(
                sg_all.at[layer, me],
                sg_all.at[layer, me],
                sg_ss.at[layer, slot],
                sg_rs.at[layer, me],
                slot,
            ).wait_send()

        loop(1, DAP, small_sent)

        def db_sent(index):
            block, z = lax.div(index, 4), lax.rem(index, 4)
            slot = block * 8 + z * 2 + core

            @pl.when(slot != me)
            def _():
                remote(
                    db_send.at[layer, block, z],
                    db_recv.at[layer, mine],
                    db_ss.at[layer, index],
                    db_rs.at[layer, mine],
                    slot,
                ).wait_send()

        loop(0, DAP // 2, db_sent)

        def pair_sent(block):
            remote(
                db_pair_send.at[layer, block],
                db_pair_recv.at[layer, block],
                pair_ss.at[layer, block],
                pair_rs.at[layer, block],
                sibling,
            ).wait_send()

        loop(0, BLOCKS, pair_sent)


def per_device(pair_rep, cotangent, norm_gain, w_project, w_bias, w_out):
    w_bias_rows = jnp.pad(jnp.swapaxes(w_bias, 1, 2), ((0, 0), (0, ROWS - HEADS), (0, 0)))
    cells = (ROWS, LENGTH, CHANNELS)
    piece = (ROWS * ROWS, CHANNELS)
    bias_piece = (HEADS * ROWS, LENGTH)
    vmem = pltpu.VMEM
    sem = pltpu.SemaphoreType.DMA
    scratch = [
        vmem((2,) + cells, BF16),
        vmem((2,) + cells, BF16),
        vmem((2,) + cells, BF16),
        vmem((2,) + cells, BF16),
        vmem((2,) + cells, BF16),
        vmem((2,) + cells, BF16),
        vmem((2,) + cells, F32),
        vmem((2,) + cells, F32),
        vmem((2,) + cells, BF16),
        vmem((ROWS, BLOCKS, STACK, LENGTH), BF16),
        vmem((ROWS, LENGTH, 4 * CHANNELS), BF16),
        vmem((ROWS, CHANNELS, LENGTH), F32),
        vmem((ROWS, CHANNELS, LENGTH), F32),
        vmem((2, CHANNELS, 4 * CHANNELS), BF16),
        vmem((2, CHANNELS, CHANNELS), BF16),
        vmem((2, HEADS * ROWS, CHANNELS), F32),
        vmem((2, DAP) + bias_piece, BF16),
        vmem((STACK, LENGTH), F32),
        vmem((ROWS, BLOCK, CHANNELS), F32),
        vmem((STACK, LENGTH), F32),
        vmem((CHANNELS, 5 * CHANNELS), F32),
        vmem((ROWS * LENGTH, CHANNELS), F32),
        vmem((DAP,) + piece, BF16),
        vmem((DAP,) + piece, BF16),
        vmem((DAP,) + piece, BF16),
        vmem((DAP,) + piece, BF16),
        vmem((DAP,) + piece, BF16),
        vmem((DAP,) + piece, BF16),
        vmem((BLOCKS, 4) + bias_piece, F32),
        vmem((2, BLOCKS, 4) + bias_piece, BF16),
        vmem((2, BLOCKS, 4) + bias_piece, BF16),
        vmem((2, BLOCKS, 4) + bias_piece, BF16),
        vmem((2, DAP // 2) + bias_piece, BF16),
        vmem((2, HEADS * ROWS, CHANNELS), F32),
        vmem((2, DAP, ROWS, 3 * CHANNELS), F32),
        vmem((2, DAP, ROWS, 3 * CHANNELS), F32),
        vmem((2, DAP, ROWS, 3 * CHANNELS), F32),
        vmem((2, DAP, ROWS, CHANNELS), F32),
        sem((DAP,)),
        sem((DAP,)),
        sem((DAP,)),
        sem((DAP,)),
        sem((DAP,)),
        sem((DAP,)),
        sem((2, DAP)),
        sem((2, DAP)),
        sem((2, DAP)),
        sem((2, BLOCKS)),
        sem((2, BLOCKS)),
        sem((2, DAP // 2)),
        sem((2, DAP // 2)),
        sem((2, DAP)),
        sem((2, DAP)),
        sem((2, DAP)),
        sem((2, DAP)),
        sem((2, DAP)),
        sem((2, DAP)),
        sem((2, DAP)),
    ]
    d_pair, small, grad_project, grad_out = pl.pallas_call(
        kernel,
        out_shape=(
            jax.ShapeDtypeStruct(cells, BF16),
            jax.ShapeDtypeStruct((2, ROWS, CHANNELS), F32),
            jax.ShapeDtypeStruct((2, CHANNELS, 4 * CHANNELS), F32),
            jax.ShapeDtypeStruct((2, CHANNELS, CHANNELS), F32),
        ),
        in_specs=[pl.BlockSpec(memory_space=pltpu.VMEM)] * 6,
        out_specs=[pl.BlockSpec(memory_space=pltpu.VMEM)] * 4,
        scratch_shapes=scratch,
        compiler_params=pltpu.CompilerParams(
            collective_id=0, has_side_effects=True, vmem_limit_bytes=56 << 20
        ),
    )(pair_rep, cotangent, norm_gain, w_project, w_bias_rows, w_out)
    grad_bias = jnp.swapaxes(small[:, :HEADS], 1, 2)
    return (d_pair, small[:, HEADS], grad_project, grad_bias, grad_out)


def solution(mesh):
    in_specs = (P(("dp", "dap"), None, None), P(("dp", "dap"), None, None), P(), P(), P(), P())
    out_specs = (
        P(("dp", "dap"), None, None),
        P("dp", None),
        P("dp", None, None),
        P("dp", None, None),
        P("dp", None, None),
    )
    return jax.shard_map(
        per_device, mesh=mesh, in_specs=in_specs, out_specs=out_specs, check_vma=False
    )
```

```python
import jax
import jax.numpy as jnp
from jax import lax
from jax.experimental import pallas as pl
from jax.experimental.pallas import tpu as pltpu
from jax.sharding import PartitionSpec as P

EPS = 1e-05
MESH = pl.DeviceIdType.MESH
F32 = jnp.float32
BF16 = jnp.bfloat16
DAP = 32
ROWS = 8
LENGTH = 256
CHANNELS = 128
HEADS = 4
BLOCKS = 4
BLOCK = LENGTH // BLOCKS
STACK = HEADS * BLOCK
SCALE = (CHANNELS // HEADS) ** (-0.5)


def slot_of(device):
    return (
        lax.rem(lax.div(device, 2), 4) * 8 + lax.div(device, 8) * 2 + lax.rem(device, 2)
    )


def device_of(slot):
    return lax.rem(lax.div(slot, 2), 4) * 8 + lax.div(slot, 8) * 2 + lax.rem(slot, 2)


def remote(src, dst, send_sem, recv_sem, slot):
    return pltpu.make_async_remote_copy(
        src_ref=src,
        dst_ref=dst,
        send_sem=send_sem,
        recv_sem=recv_sem,
        device_id=(lax.axis_index("dp"), device_of(slot)),
        device_id_type=MESH,
    )


def loop(low, high, body, unroll=1):
    def step(index, carry):
        body(index)
        return carry

    lax.fori_loop(low, high, step, 0, unroll=unroll)


def dot(a, b):
    return lax.dot_general(a, b, (((1,), (0,)), ((), ())), preferred_element_type=F32)


def dot_nt(a, b):
    return lax.dot_general(a, b, (((1,), (1,)), ((), ())), preferred_element_type=F32)


def dot_tn(a, b):
    return lax.dot_general(a, b, (((0,), (0,)), ((), ())), preferred_element_type=F32)


def centre(values):
    centred = values - jnp.mean(values, axis=-1, keepdims=True)
    variance = jnp.mean(centred * centred, axis=-1, keepdims=True)
    inverse = lax.rsqrt(variance + EPS)
    return centred * inverse, inverse


def kernel(
    x_ref,
    cot_ref,
    gain_ref,
    wp_ref,
    wb_ref,
    wo_ref,
    dpair_ref,
    small_ref,
    gproj_ref,
    gout_ref,
    rows_s,
    dy_s,
    norm_s,
    q_s,
    k_s,
    v_s,
    gate_s,
    o_s,
    mix_s,
    p_s,
    dproj_s,
    dkt_s,
    dvt_s,
    wp_s,
    wo_s,
    bias_f,
    bias_all,
    bias_q,
    dm_s,
    dbias_acc,
    wide_s,
    stage_s,
    cot_send,
    cot_recv,
    mid_send,
    mid_recv,
    back_send,
    back_recv,
    db_kept,
    db_pair_send,
    db_pair_recv,
    db_send,
    db_recv,
    db_s,
    dn_s,
    wg_half,
    wg_held,
    wg_tot,
    wg_recv,
    wg_all,
    sg_all,
    cot_ss,
    cot_rs,
    mid_ss,
    mid_rs,
    back_ss,
    back_rs,
    bias_ss,
    bias_fs,
    bias_rs,
    pair_ss,
    pair_rs,
    db_ss,
    db_rs,
    wg_ps,
    wg_ss,
    wg_rs,
    wa_ss,
    wa_fs,
    wa_rs,
    sg_ss,
    sg_rs,
):
    me = slot_of(lax.axis_index("dap"))
    mine = lax.div(me, 2)
    core = lax.rem(me, 2)
    sibling = me + 1 - 2 * core
    first_block = lax.div(me, 8)
    barrier = pltpu.get_barrier_semaphore()

    def other(step):
        return lax.rem(me + step, DAP)

    def tell(step):
        pl.semaphore_signal(
            barrier,
            inc=1,
            device_id=(lax.axis_index("dp"), device_of(other(step))),
            device_id_type=MESH,
        )

    loop(1, DAP, tell)

    lane_head = lax.div(lax.broadcasted_iota(jnp.int32, (1, CHANNELS), 1), CHANNELS // HEADS)
    masks = [jnp.where(lane_head == head, 1.0, 0.0).astype(F32) for head in range(HEADS)]
    masks_short = [mask.astype(BF16) for mask in masks]

    def stack(block):
        return jnp.concatenate([block * mask for mask in masks_short], axis=0)

    def pick(stacked):
        out = stacked[:BLOCK] * masks[0]
        for head in range(1, HEADS):
            out = out + stacked[head * BLOCK : (head + 1) * BLOCK] * masks[head]
        return out

    def block_rows(block):
        return pl.ds(pl.multiple_of(block * BLOCK, BLOCK), BLOCK)

    def gather_start(buf, ss, rs):
        remote(buf.at[me], buf.at[me], ss.at[sibling], rs.at[me], sibling).start()

        def go(step):
            slot = other(2 * step)
            remote(buf.at[me], buf.at[me], ss.at[slot], rs.at[me], slot).start()

        loop(1, DAP // 2, go)

    def gather_finish(buf, ss, fs, rs):
        def forward(step):
            slot = other(DAP - 2 * step)
            remote(buf.at[slot], buf.at[slot], ss.at[slot], rs.at[slot], slot).wait_recv()
            remote(buf.at[slot], buf.at[slot], fs.at[slot], rs.at[slot], sibling).start()

        loop(1, DAP // 2, forward)

        def take(chip):
            slot = 2 * chip + 1 - core
            remote(buf.at[slot], buf.at[slot], ss.at[slot], rs.at[slot], slot).wait_recv()

        loop(0, DAP // 2, take)

    def gather_sent(buf, ss, fs, rs):
        remote(buf.at[me], buf.at[me], ss.at[sibling], rs.at[me], sibling).wait_send()

        def done(step):
            slot = other(2 * step)
            remote(buf.at[me], buf.at[me], ss.at[slot], rs.at[me], slot).wait_send()
            remote(buf.at[slot], buf.at[slot], fs.at[slot], rs.at[slot], sibling).wait_send()

        loop(1, DAP // 2, done)

    def swap_start(send, recv, ss, rs, slot):
        @pl.when(slot != me)
        def _():
            remote(send.at[slot], recv.at[me], ss.at[slot], rs.at[me], slot).start()

    def swap_take(send, recv, ss, rs, slot):
        @pl.when(slot != me)
        def _():
            remote(send.at[slot], recv.at[slot], ss.at[slot], rs.at[slot], slot).wait_recv()

    def swap_sent(send, recv, ss, rs):
        def done(step):
            slot = other(step)
            remote(send.at[slot], recv.at[me], ss.at[slot], rs.at[me], slot).wait_send()

        loop(1, DAP, done)

    def normalise(layer, index, at, values):
        hat, _ = centre(values)
        norm_s[layer, index, at, :] = (hat * gain_ref[layer : layer + 1, :]).astype(BF16)

    def bias_start(layer):
        weight = wb_ref[layer].astype(BF16)

        def row(index):
            bias = dot_nt(weight, norm_s[layer, index])
            for half in range(2):
                bias_f[half, pl.ds(index, HEADS, stride=ROWS), :] = bias[
                    :HEADS, half * CHANNELS : (half + 1) * CHANNELS
                ]

        loop(0, ROWS, row, ROWS)
        bias_all[layer, me] = jnp.concatenate([bias_f[0], bias_f[1]], axis=1).astype(BF16)

    def project(layer):
        def row(index):
            projected = dot(norm_s[layer, index], wp_s[layer])
            q_s[layer, index] = (projected[:, :CHANNELS] * SCALE).astype(BF16)
            k_s[layer, index] = projected[:, CHANNELS : 2 * CHANNELS].astype(BF16)
            v_s[layer, index] = projected[:, 2 * CHANNELS : 3 * CHANNELS].astype(BF16)
            gate_s[layer, index] = 1.0 / (1.0 + jnp.exp(-projected[:, 3 * CHANNELS :]))

        loop(0, ROWS, row, ROWS)

    def spread_bias(layer, block):
        for part in range(8):
            piece = bias_all[layer, block * 8 + part].astype(F32)
            for head in range(HEADS):
                at = head * BLOCK + part * ROWS
                bias_q[at : at + ROWS, :] = piece[head * ROWS : (head + 1) * ROWS]

    def weights(layer, index, block):
        queries = stack(q_s[layer, index, block_rows(block), :])
        scores = dot_nt(queries, k_s[layer, index]) + bias_q[...]
        shifted = jnp.exp(scores - jnp.max(scores, axis=-1, keepdims=True))
        return queries, shifted * (1.0 / jnp.sum(shifted, axis=-1, keepdims=True))

    def mix(layer, index, block, short):
        mixed = pick(dot(short, v_s[layer, index]))
        o_s[layer, index, block_rows(block), :] = mixed
        gate = gate_s[layer, index, block_rows(block), :]
        mix_s[layer, index, block_rows(block), :] = (mixed * gate).astype(BF16)
        return mixed

    def backward(layer, load_dy, between):
        dkt_s[...] = jnp.zeros(dkt_s.shape, F32)
        dvt_s[...] = jnp.zeros(dvt_s.shape, F32)

        def pass_on(block):
            remote(
                db_pair_send.at[layer, block],
                db_pair_recv.at[layer, block],
                pair_ss.at[layer, block],
                pair_rs.at[layer, block],
                sibling,
            ).wait_recv()
            for z in range(4):
                total = db_kept[block, z] + db_pair_recv[layer, block, z].astype(F32)
                db_send[layer, block, z] = total.astype(BF16)
                slot = block * 8 + z * 2 + core

                @pl.when(slot != me)
                def _():
                    remote(
                        db_send.at[layer, block, z],
                        db_recv.at[layer, mine],
                        db_ss.at[layer, block * 4 + z],
                        db_rs.at[layer, mine],
                        slot,
                    ).start()

                @pl.when(slot == me)
                def _():
                    db_recv[layer, mine] = db_send[layer, block, z]

        def step_block(step):
            block = lax.rem(first_block + step, BLOCKS)
            load_dy(block)
            between(step)
            dy = dy_s[layer, :, block_rows(block), :].reshape(ROWS * BLOCK, CHANNELS)
            dm_s[...] = dot_nt(dy, wo_s[layer]).astype(BF16).astype(F32).reshape(dm_s.shape)
            spread_bias(layer, block)
            dbias_acc[...] = jnp.zeros(dbias_acc.shape, F32)

            def row(index):
                at = block_rows(block)
                if layer == 0:
                    queries = stack(q_s[layer, index, at, :])
                    short = p_s[index, block]
                    soft = short.astype(F32)
                    mixed = o_s[layer, index, at, :]
                else:
                    queries, soft = weights(layer, index, block)
                    short = soft.astype(BF16)
                    mixed = mix(layer, index, block, short)
                gate = gate_s[layer, index, at, :]
                dm = dm_s[index]
                d_gate = dm * mixed * gate * (1.0 - gate)
                dproj_s[index, at, 3 * CHANNELS :] = d_gate.astype(BF16)
                d_mixed = stack((dm * gate).astype(BF16))
                d_soft = dot_nt(d_mixed, v_s[layer, index]).astype(BF16).astype(F32)
                product = soft * d_soft
                d_scores = product - soft * jnp.sum(product, axis=-1, keepdims=True)
                dbias_acc[...] += d_scores
                d_short = d_scores.astype(BF16)
                d_query = pick(dot(d_short, k_s[layer, index])).astype(BF16).astype(F32)
                dproj_s[index, at, :CHANNELS] = (d_query * SCALE).astype(BF16)
                dkt_s[index] += dot_tn(queries, d_short)
                dvt_s[index] += dot_tn(d_mixed, short)

            loop(0, ROWS, row, ROWS)
            for z in range(4):
                for half in range(2):
                    part = z * 2 + half
                    piece = jnp.concatenate(
                        [
                            dbias_acc[
                                head * BLOCK + part * ROWS : head * BLOCK + (part + 1) * ROWS, :
                            ]
                            for head in range(HEADS)
                        ],
                        axis=0,
                    )

                    @pl.when(core == half)
                    def _():
                        db_kept[block, z] = piece

                    @pl.when(core != half)
                    def _():
                        db_pair_send[layer, block, z] = piece.astype(BF16)

            remote(
                db_pair_send.at[layer, block],
                db_pair_recv.at[layer, block],
                pair_ss.at[layer, block],
                pair_rs.at[layer, block],
                sibling,
            ).start()

            @pl.when(step > 0)
            def _():
                pass_on(lax.rem(first_block + step + BLOCKS - 1, BLOCKS))

        loop(0, BLOCKS, step_block)
        pass_on(lax.rem(first_block + BLOCKS - 1, BLOCKS))
        wide_s[...] = jnp.zeros(wide_s.shape, F32)

        def row_grads(index):
            dproj_s[index, :, CHANNELS : 2 * CHANNELS] = dkt_s[index].T.astype(BF16)
            dproj_s[index, :, 2 * CHANNELS : 3 * CHANNELS] = dvt_s[index].T.astype(BF16)
            wide_s[:, : 4 * CHANNELS] += dot_tn(norm_s[layer, index], dproj_s[index])
            wide_s[:, 4 * CHANNELS :] += dot_tn(mix_s[layer, index], dy_s[layer, index])

        loop(0, ROWS, row_grads, ROWS)
        for half in range(2):
            at = half * 2 * CHANNELS
            wg_half[layer, half, :, : 2 * CHANNELS] = wide_s[:, at : at + 2 * CHANNELS]
            wg_half[layer, half, :, 2 * CHANNELS :] = wide_s[:, 4 * CHANNELS :]
        wg_pair(layer).start()

        def main(index):
            dn_s[index] = dot_nt(dproj_s[index], wp_s[layer])

        loop(0, ROWS, main, ROWS)

    def wg_pair(layer):
        return remote(
            wg_half.at[layer, 1 - core],
            wg_held.at[layer],
            wg_ps.at[layer, 0],
            wg_ps.at[layer, 1],
            sibling,
        )

    def tile(slot):
        return pl.ds(pl.multiple_of(lax.div(slot, 2) * ROWS, ROWS), ROWS)

    def wg_copy(layer, slot, chip):
        return remote(
            wg_tot.at[layer, tile(slot), :],
            wg_recv.at[layer, chip],
            wg_ss.at[layer, lax.div(slot, 2)],
            wg_rs.at[layer, chip],
            slot,
        )

    def wg_start(layer):
        wg_pair(layer).wait_recv()
        wg_tot[layer] = wg_half[layer, core] + wg_held[layer]

        def go(step):
            wg_copy(layer, other(2 * step), mine).start()

        loop(1, DAP // 2, go)
        wg_recv[layer, mine] = wg_tot[layer, tile(me), :]

    def finish_bias(layer):
        def take(chip):
            @pl.when(chip != mine)
            def _():
                remote(
                    db_send.at[layer, 0, 0],
                    db_recv.at[layer, chip],
                    db_ss.at[layer, chip],
                    db_rs.at[layer, chip],
                    sibling,
                ).wait_recv()

        loop(0, DAP // 2, take)
        total = lax.fori_loop(
            0,
            DAP // 2,
            lambda chip, total: total + db_recv[layer, chip].astype(F32),
            jnp.zeros((HEADS * ROWS, LENGTH), F32),
        )
        for half in range(2):
            db_s[half] = (
                total[:, half * CHANNELS : (half + 1) * CHANNELS].astype(BF16).astype(F32)
            )

    def input_grads(layer, direction, emit, emitted):
        finish_bias(layer)
        zero = jnp.zeros((ROWS, CHANNELS), F32)
        weight = wb_ref[layer].astype(BF16)
        gain = gain_ref[layer : layer + 1, :]

        def add_bias(index, total):
            at = pl.ds(index, HEADS, stride=ROWS)
            rows = jnp.concatenate([db_s[0, at, :], db_s[1, at, :]], axis=1)
            rows = jnp.concatenate([rows, jnp.zeros((ROWS - HEADS, LENGTH), F32)], axis=0)
            rows = rows.astype(BF16)
            dn_s[index] += dot_tn(rows, weight)
            return total + dot(rows, norm_s[layer, index])

        grad_bias = lax.fori_loop(0, ROWS, add_bias, zero, unroll=ROWS)

        def step_block(step, total):
            block = lax.rem(first_block + direction * step, BLOCKS)
            at = block_rows(block)

            def row(index, total):
                d_normed = dn_s[index, at, :]
                hat, inverse = centre(rows_s[layer, index, at, :].astype(F32))
                d_hat = d_normed * gain
                d_input = inverse * (
                    d_hat
                    - jnp.mean(d_hat, axis=-1, keepdims=True)
                    - hat * jnp.mean(d_hat * hat, axis=-1, keepdims=True)
                )
                emit(block, index, dy_s[layer, index, at, :].astype(F32) + d_input)
                return total + jnp.sum(d_normed * hat, axis=0, keepdims=True)

            total = lax.fori_loop(0, ROWS, row, total, unroll=ROWS)
            emitted(block)
            return total

        grad_gain = lax.fori_loop(0, BLOCKS, step_block, jnp.zeros((1, CHANNELS), F32))
        sg_all[layer, me] = jnp.concatenate(
            [grad_bias[:HEADS], grad_gain, zero[: ROWS - HEADS - 1]], axis=0
        )

    def small_copy(layer, slot, from_slot):
        return remote(
            sg_all.at[layer, from_slot],
            sg_all.at[layer, from_slot],
            sg_ss.at[layer, slot],
            sg_rs.at[layer, from_slot],
            slot,
        )

    def small_start(layer):
        loop(1, DAP, lambda step: small_copy(layer, other(step), me).start())

    def weight_sums(layer):
        def take(step):
            slot = other(DAP - 2 * step)
            wg_copy(layer, slot, lax.div(slot, 2)).wait_recv()

        loop(1, DAP // 2, take)
        total = wg_recv[layer, 0]
        for chip in range(1, DAP // 2):
            total = total + wg_recv[layer, chip]
        wg_all[layer, me] = total
        gather_start(wg_all.at[layer], wa_ss.at[layer], wa_rs.at[layer])

    def weight_out(layer):
        gather_finish(wg_all.at[layer], wa_ss.at[layer], wa_fs.at[layer], wa_rs.at[layer])

        def place(chip):
            at = pl.ds(pl.multiple_of(chip * 8, 8), 8)
            gproj_ref[layer, at, : 2 * CHANNELS] = wg_all[layer, 2 * chip, :, : 2 * CHANNELS]
            gproj_ref[layer, at, 2 * CHANNELS :] = wg_all[layer, 2 * chip + 1, :, : 2 * CHANNELS]
            gout_ref[layer, at, :] = wg_all[layer, 2 * chip, :, 2 * CHANNELS :]

        loop(0, DAP // 2, place)

        def take(step):
            slot = other(DAP - step)
            small_copy(layer, slot, slot).wait_recv()

        loop(1, DAP, take)
        small_ref[layer] = lax.fori_loop(
            0,
            DAP,
            lambda slot, total: total + sg_all[layer, slot],
            jnp.zeros((ROWS, CHANNELS), F32),
        )

    for layer in range(2):
        wp_s[layer] = wp_ref[layer].astype(BF16)
        wo_s[layer] = wo_ref[layer].astype(BF16)
    for y in range(4):
        for z in range(4):
            rows_s[0, :, y * 64 + z * 16 : y * 64 + z * 16 + 16, :] = x_ref[
                :, z * 64 + y * 16 : z * 64 + y * 16 + 16, :
            ]
    whole = pl.ds(0, LENGTH)
    loop(0, ROWS, lambda index: normalise(0, index, whole, rows_s[0, index].astype(F32)), ROWS)
    bias_start(0)
    project(0)
    stage_s[...] = cot_ref[...].astype(F32).reshape(stage_s.shape)

    def stage_cot(slot):
        at = device_of(slot) * ROWS
        cot_send[slot] = jnp.concatenate(
            [
                stage_s[pl.ds(pl.multiple_of(row * LENGTH + at, ROWS), ROWS), :]
                for row in range(ROWS)
            ],
            axis=0,
        ).astype(BF16)

    loop(0, DAP, stage_cot, 4)
    cot_recv[me] = cot_send[me]
    pl.semaphore_wait(barrier, DAP - 1)
    gather_start(bias_all.at[0], bias_ss.at[0], bias_rs.at[0])

    def cot_start(step):
        block = lax.rem(first_block + BLOCKS - step, BLOCKS)
        loop(
            0,
            8,
            lambda part: swap_start(cot_send, cot_recv, cot_ss, cot_rs, block * 8 + part),
        )

    cot_start(0)
    gather_finish(bias_all.at[0], bias_ss.at[0], bias_fs.at[0], bias_rs.at[0])

    def forward_block(step):
        block = lax.rem(first_block + step, BLOCKS)
        spread_bias(0, block)

        def row(index):
            _, soft = weights(0, index, block)
            short = soft.astype(BF16)
            p_s[index, block] = short
            mix(0, index, block, short)

        loop(0, ROWS, row, ROWS)
        mixture = mix_s[0, :, block_rows(block), :].reshape(ROWS * BLOCK, CHANNELS)
        term = dot(mixture, wo_s[0]).reshape(ROWS, BLOCK, CHANNELS)
        middle = rows_s[0, :, block_rows(block), :].astype(F32) + term
        for part in range(8):
            slot = block * 8 + part
            mid_send[slot] = (
                middle[:, part * ROWS : (part + 1) * ROWS, :]
                .reshape(ROWS * ROWS, CHANNELS)
                .astype(BF16)
            )
            swap_start(mid_send, mid_recv, mid_ss, mid_rs, slot)

    loop(0, BLOCKS, forward_block)
    mid_recv[me] = mid_send[me]

    def chunk(block, index):
        return pl.ds(block * (BLOCK * ROWS) + index, BLOCK, stride=ROWS)

    def unpack(recv, block):
        at = pl.ds(pl.multiple_of(block * (BLOCK * ROWS), BLOCK * ROWS), BLOCK * ROWS)
        pieces = recv[pl.ds(pl.multiple_of(block * 8, 8), 8)]
        stage_s[at, :] = pieces.astype(F32).reshape(BLOCK * ROWS, CHANNELS)

    def middle_block(step):
        block = lax.rem(first_block + BLOCKS - step, BLOCKS)
        loop(
            0,
            8,
            lambda part: swap_take(mid_send, mid_recv, mid_ss, mid_rs, block * 8 + part),
        )
        unpack(mid_recv, block)

        def row(index):
            values = stage_s[chunk(block, index), :]
            rows_s[1, index, block_rows(block), :] = values.astype(BF16)
            normalise(1, index, block_rows(block), values)

        loop(0, ROWS, row, ROWS)

    loop(0, BLOCKS, middle_block)
    bias_start(1)
    gather_start(bias_all.at[1], bias_ss.at[1], bias_rs.at[1])
    project(1)
    loop(1, BLOCKS, cot_start)
    gather_finish(bias_all.at[1], bias_ss.at[1], bias_fs.at[1], bias_rs.at[1])

    def load_cot(block):
        loop(
            0,
            8,
            lambda part: swap_take(cot_send, cot_recv, cot_ss, cot_rs, block * 8 + part),
        )
        unpack(cot_recv, block)
        for index in range(ROWS):
            dy_s[1, index, block_rows(block), :] = stage_s[chunk(block, index), :].astype(BF16)

    backward(1, load_cot, lambda step: None)

    def emit_back(block, index, values):
        stage_s[chunk(block, index), :] = values

    def back_start(block):
        for part in range(8):
            slot = block * 8 + part
            at = pl.ds(pl.multiple_of(slot * (ROWS * ROWS), ROWS * ROWS), ROWS * ROWS)
            back_send[slot] = stage_s[at, :].astype(BF16)
            swap_start(back_send, back_recv, back_ss, back_rs, slot)

    input_grads(1, BLOCKS - 1, emit_back, back_start)
    back_recv[me] = back_send[me]

    def load_back(block):
        loop(
            0,
            8,
            lambda part: swap_take(back_send, back_recv, back_ss, back_rs, block * 8 + part),
        )
        pieces = [
            back_recv[block * 8 + part].astype(F32).reshape(ROWS, ROWS, CHANNELS)
            for part in range(8)
        ]
        dy_s[0, :, block_rows(block), :] = jnp.concatenate(pieces, axis=1).astype(BF16)

    def sum_layer_one(step):
        @pl.when(step == 1)
        def _():
            small_start(1)
            wg_start(1)

        @pl.when(step == 3)
        def _():
            weight_sums(1)

    backward(0, load_back, sum_layer_one)
    wg_start(0)

    def emit_pair(block, index, values):
        short = values.astype(BF16)
        for z in range(4):
            at = pl.ds(pl.multiple_of(z * 64 + block * 16, 16), 16)
            dpair_ref[index, at, :] = short[z * 16 : z * 16 + 16]

    input_grads(0, 1, emit_pair, lambda block: None)
    small_start(0)
    weight_sums(0)
    weight_out(1)
    weight_out(0)

    swap_sent(cot_send, cot_recv, cot_ss, cot_rs)
    swap_sent(mid_send, mid_recv, mid_ss, mid_rs)
    swap_sent(back_send, back_recv, back_ss, back_rs)
    for layer in range(2):
        gather_sent(bias_all.at[layer], bias_ss.at[layer], bias_fs.at[layer], bias_rs.at[layer])
        gather_sent(wg_all.at[layer], wa_ss.at[layer], wa_fs.at[layer], wa_rs.at[layer])
        wg_pair(layer).wait_send()
        loop(1, DAP // 2, lambda step: wg_copy(layer, other(2 * step), mine).wait_send())
        loop(1, DAP, lambda step: small_copy(layer, other(step), me).wait_send())

        def db_sent(index):
            block, z = lax.div(index, 4), lax.rem(index, 4)
            slot = block * 8 + z * 2 + core

            @pl.when(slot != me)
            def _():
                remote(
                    db_send.at[layer, block, z],
                    db_recv.at[layer, mine],
                    db_ss.at[layer, index],
                    db_rs.at[layer, mine],
                    slot,
                ).wait_send()

        loop(0, DAP // 2, db_sent)

        def pair_sent(block):
            remote(
                db_pair_send.at[layer, block],
                db_pair_recv.at[layer, block],
                pair_ss.at[layer, block],
                pair_rs.at[layer, block],
                sibling,
            ).wait_send()

        loop(0, BLOCKS, pair_sent)


def per_device(pair_rep, cotangent, norm_gain, w_project, w_bias, w_out):
    w_bias_rows = jnp.pad(jnp.swapaxes(w_bias, 1, 2), ((0, 0), (0, ROWS - HEADS), (0, 0)))
    cells = (ROWS, LENGTH, CHANNELS)
    piece = (ROWS * ROWS, CHANNELS)
    bias_piece = (HEADS * ROWS, LENGTH)
    vmem = pltpu.VMEM
    sem = pltpu.SemaphoreType.DMA
    scratch = [
        vmem((2,) + cells, BF16),
        vmem((2,) + cells, BF16),
        vmem((2,) + cells, BF16),
        vmem((2,) + cells, BF16),
        vmem((2,) + cells, BF16),
        vmem((2,) + cells, BF16),
        vmem((2,) + cells, F32),
        vmem((2,) + cells, F32),
        vmem((2,) + cells, BF16),
        vmem((ROWS, BLOCKS, STACK, LENGTH), BF16),
        vmem((ROWS, LENGTH, 4 * CHANNELS), BF16),
        vmem((ROWS, CHANNELS, LENGTH), F32),
        vmem((ROWS, CHANNELS, LENGTH), F32),
        vmem((2, CHANNELS, 4 * CHANNELS), BF16),
        vmem((2, CHANNELS, CHANNELS), BF16),
        vmem((2, HEADS * ROWS, CHANNELS), F32),
        vmem((2, DAP) + bias_piece, BF16),
        vmem((STACK, LENGTH), F32),
        vmem((ROWS, BLOCK, CHANNELS), F32),
        vmem((STACK, LENGTH), F32),
        vmem((CHANNELS, 5 * CHANNELS), F32),
        vmem((ROWS * LENGTH, CHANNELS), F32),
        vmem((DAP,) + piece, BF16),
        vmem((DAP,) + piece, BF16),
        vmem((DAP,) + piece, BF16),
        vmem((DAP,) + piece, BF16),
        vmem((DAP,) + piece, BF16),
        vmem((DAP,) + piece, BF16),
        vmem((BLOCKS, 4) + bias_piece, F32),
        vmem((2, BLOCKS, 4) + bias_piece, BF16),
        vmem((2, BLOCKS, 4) + bias_piece, BF16),
        vmem((2, BLOCKS, 4) + bias_piece, BF16),
        vmem((2, DAP // 2) + bias_piece, BF16),
        vmem((2, HEADS * ROWS, CHANNELS), F32),
        vmem(cells, F32),
        vmem((2, 2, CHANNELS, 3 * CHANNELS), F32),
        vmem((2, CHANNELS, 3 * CHANNELS), F32),
        vmem((2, CHANNELS, 3 * CHANNELS), F32),
        vmem((2, DAP // 2, ROWS, 3 * CHANNELS), F32),
        vmem((2, DAP, ROWS, 3 * CHANNELS), F32),
        vmem((2, DAP, ROWS, CHANNELS), F32),
        sem((DAP,)),
        sem((DAP,)),
        sem((DAP,)),
        sem((DAP,)),
        sem((DAP,)),
        sem((DAP,)),
        sem((2, DAP)),
        sem((2, DAP)),
        sem((2, DAP)),
        sem((2, BLOCKS)),
        sem((2, BLOCKS)),
        sem((2, DAP // 2)),
        sem((2, DAP // 2)),
        sem((2, 2)),
        sem((2, DAP // 2)),
        sem((2, DAP // 2)),
        sem((2, DAP)),
        sem((2, DAP)),
        sem((2, DAP)),
        sem((2, DAP)),
        sem((2, DAP)),
    ]
    d_pair, small, grad_project, grad_out = pl.pallas_call(
        kernel,
        out_shape=(
            jax.ShapeDtypeStruct(cells, BF16),
            jax.ShapeDtypeStruct((2, ROWS, CHANNELS), F32),
            jax.ShapeDtypeStruct((2, CHANNELS, 4 * CHANNELS), F32),
            jax.ShapeDtypeStruct((2, CHANNELS, CHANNELS), F32),
        ),
        in_specs=[pl.BlockSpec(memory_space=pltpu.VMEM)] * 6,
        out_specs=[pl.BlockSpec(memory_space=pltpu.VMEM)] * 4,
        scratch_shapes=scratch,
        compiler_params=pltpu.CompilerParams(
            collective_id=0, has_side_effects=True, vmem_limit_bytes=56 << 20
        ),
    )(pair_rep, cotangent, norm_gain, w_project, w_bias_rows, w_out)
    grad_bias = jnp.swapaxes(small[:, :HEADS], 1, 2)
    return (d_pair, small[:, HEADS], grad_project, grad_bias, grad_out)


def solution(mesh):
    in_specs = (P(("dp", "dap"), None, None), P(("dp", "dap"), None, None), P(), P(), P(), P())
    out_specs = (
        P(("dp", "dap"), None, None),
        P("dp", None),
        P("dp", None, None),
        P("dp", None, None),
        P("dp", None, None),
    )
    return jax.shard_map(
        per_device, mesh=mesh, in_specs=in_specs, out_specs=out_specs, check_vma=False
    )
```

```python
import jax
import jax.numpy as jnp
from jax import lax
from jax.experimental import pallas as pl
from jax.experimental.pallas import tpu as pltpu
from jax.sharding import PartitionSpec as P

EPS = 1e-05
MESH = pl.DeviceIdType.MESH
F32 = jnp.float32
BF16 = jnp.bfloat16
DAP = 32
ROWS = 8
LENGTH = 256
CHANNELS = 128
HEADS = 4
BLOCKS = 4
BLOCK = LENGTH // BLOCKS
STACK = HEADS * BLOCK
SCALE = (CHANNELS // HEADS) ** (-0.5)


def slot_of(device):
    return (
        lax.rem(lax.div(device, 2), 4) * 8 + lax.div(device, 8) * 2 + lax.rem(device, 2)
    )


def device_of(slot):
    return lax.rem(lax.div(slot, 2), 4) * 8 + lax.div(slot, 8) * 2 + lax.rem(slot, 2)


def remote(src, dst, send_sem, recv_sem, slot):
    return pltpu.make_async_remote_copy(
        src_ref=src,
        dst_ref=dst,
        send_sem=send_sem,
        recv_sem=recv_sem,
        device_id=(lax.axis_index("dp"), device_of(slot)),
        device_id_type=MESH,
    )


def loop(low, high, body, unroll=1):
    def step(index, carry):
        body(index)
        return carry

    lax.fori_loop(low, high, step, 0, unroll=unroll)


def dot(a, b):
    return lax.dot_general(a, b, (((1,), (0,)), ((), ())), preferred_element_type=F32)


def dot_nt(a, b):
    return lax.dot_general(a, b, (((1,), (1,)), ((), ())), preferred_element_type=F32)


def dot_tn(a, b):
    return lax.dot_general(a, b, (((0,), (0,)), ((), ())), preferred_element_type=F32)


def centre(values):
    centred = values - jnp.mean(values, axis=-1, keepdims=True)
    variance = jnp.mean(centred * centred, axis=-1, keepdims=True)
    inverse = lax.rsqrt(variance + EPS)
    return centred * inverse, inverse


def kernel(
    x_hbm,
    cot_hbm,
    gain_hbm,
    wp_hbm,
    wb_hbm,
    wo_hbm,
    dpair_hbm,
    small_ref,
    gproj_hbm,
    gout_hbm,
    x_ref,
    cot_ref,
    gain_ref,
    wp_ref,
    wb_ref,
    wo_ref,
    dpair_ref,
    gproj_ref,
    gout_ref,
    in_s,
    out_s,
    rows_s,
    dy_s,
    norm_s,
    q_s,
    k_s,
    v_s,
    gate_s,
    o_s,
    mix_s,
    p_s,
    dproj_s,
    dkt_s,
    dvt_s,
    wp_s,
    wo_s,
    wb_s,
    bias_f,
    bias_all,
    bias_two,
    bias_q,
    dm_s,
    dbias_acc,
    wide_s,
    stage_s,
    cot_send,
    cot_recv,
    mid_send,
    mid_recv,
    back_send,
    back_recv,
    db_kept,
    db_pair_send,
    db_pair_recv,
    db_send,
    db_recv,
    db_s,
    dn_s,
    wg_half,
    wg_held,
    wg_tot,
    wg_recv,
    wg_all,
    wy_recv,
    wy_tot,
    wz_recv,
    wg_own,
    wg_other,
    sg_all,
    cot_ss,
    cot_rs,
    mid_ss,
    mid_rs,
    back_ss,
    back_rs,
    bias_ss,
    bias_rs,
    far_ss,
    far_rs,
    pass_ss,
    pass_rs,
    pair_ss,
    pair_rs,
    db_ss,
    db_rs,
    wg_ps,
    st_ss,
    st_rs,
    wg_ss,
    wg_rs,
    sg_ss,
    sg_rs,
):
    me = slot_of(lax.axis_index("dap"))
    mine = lax.div(me, 2)
    core = lax.rem(me, 2)
    sibling = me + 1 - 2 * core
    first_block = lax.div(me, 8)
    barrier = pltpu.get_barrier_semaphore()

    def other(step):
        return lax.rem(me + step, DAP)

    def tell(step):
        pl.semaphore_signal(
            barrier,
            inc=1,
            device_id=(lax.axis_index("dp"), device_of(other(step))),
            device_id_type=MESH,
        )

    loop(1, DAP, tell)

    def load(src, dst, index):
        return pltpu.make_async_copy(src, dst, in_s.at[index])

    x_load = load(x_hbm, x_ref, 0)
    gain_load = load(gain_hbm, gain_ref, 1)
    wb_load = load(wb_hbm, wb_ref, 2)
    weight_loads = [load(wp_hbm, wp_ref, 3), load(wo_hbm, wo_ref, 4)]
    cot_load = load(cot_hbm, cot_ref, 5)
    for copy in [gain_load, wb_load, x_load] + weight_loads + [cot_load]:
        copy.start()

    def store(src, dst, index):
        return pltpu.make_async_copy(src, dst, out_s.at[index])

    pair_store = store(dpair_ref, dpair_hbm, 0)

    def weight_stores(layer):
        return [
            store(gproj_ref.at[layer], gproj_hbm.at[layer], 1 + layer),
            store(gout_ref.at[layer], gout_hbm.at[layer], 3 + layer),
        ]

    lane_head = lax.div(lax.broadcasted_iota(jnp.int32, (1, CHANNELS), 1), CHANNELS // HEADS)
    masks = [jnp.where(lane_head == head, 1.0, 0.0).astype(F32) for head in range(HEADS)]
    masks_short = [mask.astype(BF16) for mask in masks]

    def stack(block):
        return jnp.concatenate([block * mask for mask in masks_short], axis=0)

    def pick(stacked):
        out = stacked[:BLOCK] * masks[0]
        for head in range(1, HEADS):
            out = out + stacked[head * BLOCK : (head + 1) * BLOCK] * masks[head]
        return out

    def block_rows(block):
        return pl.ds(pl.multiple_of(block * BLOCK, BLOCK), BLOCK)

    def along_y(y):
        return y * 8 + lax.rem(me, 8)

    def turn(at, step):
        return lax.rem(at + step, 4)

    def near(step):
        return first_block * 8 + lax.rem(lax.rem(me, 8) + step, 8)

    def near_copy(layer, slot):
        return remote(
            bias_all.at[layer, me], bias_all.at[layer, me], bias_ss.at[layer], bias_rs.at[layer], slot
        )

    def near_all(layer):
        held = bias_all.at[layer, pl.ds(0, 7)]
        return remote(held, held, bias_ss.at[layer], bias_rs.at[layer], sibling)

    def far_all(layer, ss, rs):
        held = bias_all.at[layer, pl.ds(0, 12)]
        return remote(held, held, ss.at[layer], rs.at[layer], sibling)

    def half_of(y, half):
        return pl.ds(pl.multiple_of(y * 8 + half * 4, 4), 4)

    def far_copy(layer, y):
        held = bias_all.at[layer, half_of(first_block, core)]
        return remote(held, held, far_ss.at[layer], far_rs.at[layer], along_y(y))

    def far_pass(layer, y):
        held = bias_all.at[layer, half_of(y, core)]
        return remote(held, held, pass_ss.at[layer], pass_rs.at[layer], sibling)

    def near_start(layer):
        loop(1, 8, lambda step: near_copy(layer, near(step)).start())

    def far_start(layer):
        near_all(layer).wait_recv()
        loop(1, 4, lambda step: far_copy(layer, turn(first_block, step)).start())

    def far_forward(layer):
        far_all(layer, far_ss, far_rs).wait_recv()
        loop(1, 4, lambda step: far_pass(layer, turn(first_block, step)).start())

    def far_take(layer):
        far_all(layer, pass_ss, pass_rs).wait_recv()

    def bias_sent(layer):
        near_all(layer).wait_send()
        far_all(layer, far_ss, far_rs).wait_send()
        far_all(layer, pass_ss, pass_rs).wait_send()

    def swap_start(send, recv, ss, rs, slot):
        @pl.when(slot != me)
        def _():
            remote(send.at[slot], recv.at[me], ss.at[0], rs.at[first_block], slot).start()

    def swap_take(recv, ss, rs, block):
        def take(count):
            held = recv.at[pl.ds(0, count)]
            remote(held, held, ss.at[0], rs.at[block], sibling).wait_recv()

        @pl.when(block == first_block)
        def _():
            take(7)

        @pl.when(block != first_block)
        def _():
            take(8)

    def swap_sent(send, ss, rs):
        held = send.at[pl.ds(0, DAP - 1)]
        remote(held, held, ss.at[0], rs.at[0], sibling).wait_send()

    def normalise(layer, index, at, values):
        hat, _ = centre(values)
        norm_s[layer, index, at, :] = (hat * gain_ref[layer : layer + 1, :]).astype(BF16)

    def bias_start(layer):
        weight = wb_s[layer].astype(BF16)

        def row(index):
            bias = dot_nt(weight, norm_s[layer, index])
            for half in range(2):
                bias_f[half, pl.ds(index, HEADS, stride=ROWS), :] = bias[
                    :HEADS, half * CHANNELS : (half + 1) * CHANNELS
                ]

        loop(0, ROWS, row, ROWS)
        bias_all[layer, me] = jnp.concatenate([bias_f[0], bias_f[1]], axis=1).astype(BF16)

    def project(layer):
        def row(index):
            projected = dot(norm_s[layer, index], wp_s[layer])
            q_s[layer, index] = (projected[:, :CHANNELS] * SCALE).astype(BF16)
            k_s[layer, index] = projected[:, CHANNELS : 2 * CHANNELS].astype(BF16)
            v_s[layer, index] = projected[:, 2 * CHANNELS : 3 * CHANNELS].astype(BF16)
            gate_s[layer, index] = 1.0 / (1.0 + jnp.exp(-projected[:, 3 * CHANNELS :]))

        loop(0, ROWS, row, ROWS)

    def spread_bias(layer, block):
        if layer == 1:
            for head in range(HEADS):
                at = head * BLOCK
                bias_q[at : at + BLOCK, :] = bias_two[head, block_rows(block), :]
            return
        for part in range(8):
            piece = bias_all[layer, block * 8 + part].astype(F32)
            for head in range(HEADS):
                at = head * BLOCK + part * ROWS
                bias_q[at : at + ROWS, :] = piece[head * ROWS : (head + 1) * ROWS]

    def weights(layer, index, block):
        queries = stack(q_s[layer, index, block_rows(block), :])
        scores = dot_nt(queries, k_s[layer, index]) + bias_q[...]
        shifted = jnp.exp(scores - jnp.max(scores, axis=-1, keepdims=True))
        return queries, shifted * (1.0 / jnp.sum(shifted, axis=-1, keepdims=True))

    def mix(layer, index, block, short):
        mixed = pick(dot(short, v_s[layer, index]))
        o_s[layer, index, block_rows(block), :] = mixed
        gate = gate_s[layer, index, block_rows(block), :]
        mix_s[layer, index, block_rows(block), :] = (mixed * gate).astype(BF16)
        return mixed

    def backward(layer, load_dy, between):
        dkt_s[...] = jnp.zeros(dkt_s.shape, F32)
        dvt_s[...] = jnp.zeros(dvt_s.shape, F32)

        def pass_on(block):
            remote(
                db_pair_send.at[layer, block],
                db_pair_recv.at[layer, block],
                pair_ss.at[layer, block],
                pair_rs.at[layer, block],
                sibling,
            ).wait_recv()
            for z in range(4):
                total = db_kept[block, z] + db_pair_recv[layer, block, z].astype(F32)
                db_send[layer, block, z] = total.astype(BF16)
                slot = block * 8 + z * 2 + core

                @pl.when(slot != me)
                def _():
                    remote(
                        db_send.at[layer, block, z],
                        db_recv.at[layer, mine],
                        db_ss.at[layer],
                        db_rs.at[layer],
                        slot,
                    ).start()

                @pl.when(slot == me)
                def _():
                    db_recv[layer, mine] = db_send[layer, block, z]

        def step_block(step):
            block = lax.rem(first_block + step, BLOCKS)
            load_dy(block)
            between(step)
            dy = dy_s[layer, :, block_rows(block), :].reshape(ROWS * BLOCK, CHANNELS)
            dm_s[...] = dot_nt(dy, wo_s[layer]).astype(BF16).astype(F32).reshape(dm_s.shape)
            spread_bias(layer, block)
            dbias_acc[...] = jnp.zeros(dbias_acc.shape, F32)

            def row(index):
                at = block_rows(block)
                if layer == 0:
                    queries = stack(q_s[layer, index, at, :])
                    short = p_s[index, block]
                    soft = short.astype(F32)
                    mixed = o_s[layer, index, at, :]
                else:
                    queries, soft = weights(layer, index, block)
                    short = soft.astype(BF16)
                    mixed = mix(layer, index, block, short)
                gate = gate_s[layer, index, at, :]
                dm = dm_s[index]
                d_gate = dm * mixed * gate * (1.0 - gate)
                dproj_s[index, at, 3 * CHANNELS :] = d_gate.astype(BF16)
                d_mixed = stack((dm * gate).astype(BF16))
                d_soft = dot_nt(d_mixed, v_s[layer, index]).astype(BF16).astype(F32)
                product = soft * d_soft
                d_scores = product - soft * jnp.sum(product, axis=-1, keepdims=True)
                dbias_acc[...] += d_scores
                d_short = d_scores.astype(BF16)
                d_query = pick(dot(d_short, k_s[layer, index])).astype(BF16).astype(F32)
                dproj_s[index, at, :CHANNELS] = (d_query * SCALE).astype(BF16)
                dkt_s[index] += dot_tn(queries, d_short)
                dvt_s[index] += dot_tn(d_mixed, short)

            loop(0, ROWS, row, ROWS)
            for z in range(4):
                for half in range(2):
                    part = z * 2 + half
                    piece = jnp.concatenate(
                        [
                            dbias_acc[
                                head * BLOCK + part * ROWS : head * BLOCK + (part + 1) * ROWS, :
                            ]
                            for head in range(HEADS)
                        ],
                        axis=0,
                    )

                    @pl.when(core == half)
                    def _():
                        db_kept[block, z] = piece

                    @pl.when(core != half)
                    def _():
                        db_pair_send[layer, block, z] = piece.astype(BF16)

            remote(
                db_pair_send.at[layer, block],
                db_pair_recv.at[layer, block],
                pair_ss.at[layer, block],
                pair_rs.at[layer, block],
                sibling,
            ).start()

            @pl.when(step > 0)
            def _():
                pass_on(lax.rem(first_block + step + BLOCKS - 1, BLOCKS))

        loop(0, BLOCKS, step_block)
        wide_s[...] = jnp.zeros(wide_s.shape, F32)

        def row_grads(index):
            dproj_s[index, :, CHANNELS : 2 * CHANNELS] = dkt_s[index].T.astype(BF16)
            dproj_s[index, :, 2 * CHANNELS : 3 * CHANNELS] = dvt_s[index].T.astype(BF16)
            wide_s[:, : 4 * CHANNELS] += dot_tn(norm_s[layer, index], dproj_s[index])
            wide_s[:, 4 * CHANNELS :] += dot_tn(mix_s[layer, index], dy_s[layer, index])

        loop(0, ROWS, row_grads, ROWS)
        pass_on(lax.rem(first_block + BLOCKS - 1, BLOCKS))
        for half in range(2):
            at = half * 2 * CHANNELS
            wg_half[layer, half, :, : 2 * CHANNELS] = wide_s[:, at : at + 2 * CHANNELS]
            wg_half[layer, half, :, 2 * CHANNELS :] = wide_s[:, 4 * CHANNELS :]
        wg_pair(layer).start()

        def main(index):
            dn_s[index] = dot_nt(dproj_s[index], wp_s[layer])

        loop(0, ROWS, main, ROWS)

    def wg_pair(layer):
        return remote(
            wg_half.at[layer, 1 - core],
            wg_held.at[layer],
            wg_ps.at[layer, 0],
            wg_ps.at[layer, 1],
            sibling,
        )

    def wg_add(layer):
        wg_pair(layer).wait_recv()
        wg_tot[layer] = wg_half[layer, core] + wg_held[layer]

    def tile(slot):
        return pl.ds(pl.multiple_of(lax.div(slot, 2) * ROWS, ROWS), ROWS)

    def wg_copy(slot):
        return remote(
            wg_tot.at[0, tile(slot), :], wg_recv.at[mine], wg_ss.at[0], wg_rs.at[0], slot
        )

    def tiles_all(held, index):
        piece = held.at[pl.ds(0, DAP // 2 - 1)]
        return remote(piece, piece, wg_ss.at[index], wg_rs.at[index], sibling)

    def wa_copy(slot):
        held = wg_all.at[core, mine]
        return remote(held, held, wg_ss.at[1], wg_rs.at[1], slot)

    def wa_pass():
        return remote(wg_all.at[core], wg_all.at[core], wg_ss.at[2], wg_rs.at[2], sibling)

    def wg_start():
        wg_add(0)
        loop(1, DAP // 2, lambda step: wg_copy(other(2 * step)).start())
        wg_recv[mine] = wg_tot[0, tile(me), :]

    my_z = lax.rem(mine, 4)

    def along_z(z):
        return first_block * 8 + z * 2 + core

    def quarter(y):
        return pl.ds(pl.multiple_of(y * 32, 32), 32)

    def eighth(y, z):
        return pl.ds(pl.multiple_of(y * 32 + z * 8, 8), 8)

    def stage_one(y):
        return remote(
            wg_tot.at[1, quarter(y), :],
            wy_recv.at[first_block],
            st_ss.at[0],
            st_rs.at[0],
            along_y(y),
        )

    def stage_two(z):
        return remote(
            wy_tot.at[pl.ds(pl.multiple_of(z * 8, 8), 8), :],
            wz_recv.at[my_z],
            st_ss.at[1],
            st_rs.at[1],
            along_z(z),
        )

    def stage_three(z):
        held = wg_own.at[eighth(first_block, my_z), :]
        return remote(held, held, st_ss.at[2], st_rs.at[2], along_z(z))

    def stage_four(y):
        held = wg_own.at[quarter(first_block), :]
        return remote(held, held, st_ss.at[3], st_rs.at[3], along_y(y))

    def stage_all(index):
        rows = (3 * 32, 3 * 8, 3 * 8, 3 * 32)[index]
        held = wg_own.at[pl.ds(0, rows), :]
        return remote(held, held, st_ss.at[index], st_rs.at[index], sibling)

    def stage_five():
        return remote(wg_own, wg_other, wg_ps.at[2, 0], wg_ps.at[2, 1], sibling)

    def three(copy, at):
        loop(1, 4, lambda step: copy(turn(at, step)).start())

    def sum_layer_one(step):
        @pl.when(step == 0)
        def _():
            wg_add(1)
            three(stage_one, first_block)
            wy_recv[first_block] = wg_tot[1, quarter(first_block), :]

        @pl.when(step == 1)
        def _():
            stage_all(0).wait_recv()
            wy_tot[...] = wy_recv[0] + wy_recv[1] + wy_recv[2] + wy_recv[3]
            three(stage_two, my_z)
            wz_recv[my_z] = wy_tot[pl.ds(pl.multiple_of(my_z * 8, 8), 8), :]
            small_start(1)

        @pl.when(step == 2)
        def _():
            stage_all(1).wait_recv()
            wg_own[eighth(first_block, my_z), :] = (
                wz_recv[0] + wz_recv[1] + wz_recv[2] + wz_recv[3]
            )
            three(stage_three, my_z)

        @pl.when(step == 3)
        def _():
            stage_all(2).wait_recv()
            three(stage_four, first_block)

    def db_all(layer):
        held = db_recv.at[layer, pl.ds(0, DAP // 2 - 1)]
        return remote(held, held, db_ss.at[layer], db_rs.at[layer], sibling)

    def finish_bias(layer):
        db_all(layer).wait_recv()
        total = lax.fori_loop(
            0,
            DAP // 2,
            lambda chip, total: total + db_recv[layer, chip].astype(F32),
            jnp.zeros((HEADS * ROWS, LENGTH), F32),
        )
        for half in range(2):
            db_s[half] = (
                total[:, half * CHANNELS : (half + 1) * CHANNELS].astype(BF16).astype(F32)
            )

    def input_grads(layer, direction, emit, emitted):
        finish_bias(layer)
        zero = jnp.zeros((ROWS, CHANNELS), F32)
        weight = wb_s[layer].astype(BF16)
        gain = gain_ref[layer : layer + 1, :]

        def add_bias(index, total):
            at = pl.ds(index, HEADS, stride=ROWS)
            rows = jnp.concatenate([db_s[0, at, :], db_s[1, at, :]], axis=1)
            rows = jnp.concatenate([rows, jnp.zeros((ROWS - HEADS, LENGTH), F32)], axis=0)
            rows = rows.astype(BF16)
            dn_s[index] += dot_tn(rows, weight)
            return total + dot(rows, norm_s[layer, index])

        grad_bias = lax.fori_loop(0, ROWS, add_bias, zero, unroll=ROWS)

        def step_block(step, total):
            block = lax.rem(first_block + direction * step, BLOCKS)
            at = block_rows(block)

            def row(index, total):
                d_normed = dn_s[index, at, :]
                hat, inverse = centre(rows_s[layer, index, at, :].astype(F32))
                d_hat = d_normed * gain
                d_input = inverse * (
                    d_hat
                    - jnp.mean(d_hat, axis=-1, keepdims=True)
                    - hat * jnp.mean(d_hat * hat, axis=-1, keepdims=True)
                )
                emit(block, index, dy_s[layer, index, at, :].astype(F32) + d_input)
                return total + jnp.sum(d_normed * hat, axis=0, keepdims=True)

            total = lax.fori_loop(0, ROWS, row, total, unroll=ROWS)
            emitted(block)
            return total

        grad_gain = lax.fori_loop(0, BLOCKS, step_block, jnp.zeros((1, CHANNELS), F32))
        sg_all[layer, me] = jnp.concatenate(
            [grad_bias[:HEADS], grad_gain, zero[: ROWS - HEADS - 1]], axis=0
        )

    def small_copy(layer, slot):
        held = sg_all.at[layer, me]
        return remote(held, held, sg_ss.at[layer], sg_rs.at[layer], slot)

    def small_all(layer):
        held = sg_all.at[layer, pl.ds(0, DAP - 1)]
        return remote(held, held, sg_ss.at[layer], sg_rs.at[layer], sibling)

    def small_start(layer):
        loop(1, DAP, lambda step: small_copy(layer, other(step)).start())

    def weight_sums():
        tiles_all(wg_recv, 0).wait_recv()
        total = wg_recv[0]
        for chip in range(1, DAP // 2):
            total = total + wg_recv[chip]
        wg_all[core, mine] = total
        loop(1, DAP // 2, lambda step: wa_copy(other(2 * step)).start())

    def small_out(layer):
        small_all(layer).wait_recv()
        total = sg_all[layer, 0]
        for slot in range(1, DAP):
            total = total + sg_all[layer, slot]
        small_ref[layer] = total

    def weight_out():
        tiles_all(wg_all.at[core], 1).wait_recv()
        wa_pass().start()
        wa_pass().wait_recv()

        def place(chip):
            at = pl.ds(pl.multiple_of(chip * 8, 8), 8)
            gproj_ref[0, at, : 2 * CHANNELS] = wg_all[0, chip, :, : 2 * CHANNELS]
            gproj_ref[0, at, 2 * CHANNELS :] = wg_all[1, chip, :, : 2 * CHANNELS]
            gout_ref[0, at, :] = wg_all[0, chip, :, 2 * CHANNELS :]

        loop(0, DAP // 2, place, 4)

    def weight_out_one():
        stage_five().wait_recv()
        gout_ref[1] = wg_own[:, 2 * CHANNELS :]

        @pl.when(core == 0)
        def _():
            gproj_ref[1, :, : 2 * CHANNELS] = wg_own[:, : 2 * CHANNELS]
            gproj_ref[1, :, 2 * CHANNELS :] = wg_other[:, : 2 * CHANNELS]

        @pl.when(core == 1)
        def _():
            gproj_ref[1, :, : 2 * CHANNELS] = wg_other[:, : 2 * CHANNELS]
            gproj_ref[1, :, 2 * CHANNELS :] = wg_own[:, : 2 * CHANNELS]

    for copy in [gain_load, wb_load, x_load]:
        copy.wait()
    for layer in range(2):
        wb_s[layer] = jnp.concatenate(
            [wb_ref[layer], jnp.zeros((ROWS - HEADS, CHANNELS), F32)], axis=0
        )
    for y in range(4):
        for z in range(4):
            rows_s[0, :, y * 64 + z * 16 : y * 64 + z * 16 + 16, :] = x_ref[
                :, z * 64 + y * 16 : z * 64 + y * 16 + 16, :
            ]
    whole = pl.ds(0, LENGTH)
    loop(0, ROWS, lambda index: normalise(0, index, whole, rows_s[0, index].astype(F32)), ROWS)
    bias_start(0)
    for copy in weight_loads:
        copy.wait()
    for layer in range(2):
        wp_s[layer] = wp_ref[layer].astype(BF16)
        wo_s[layer] = wo_ref[layer].astype(BF16)
    project(0)
    cot_load.wait()
    stage_s[...] = cot_ref[...].astype(F32).reshape(stage_s.shape)

    def stage_cot(slot):
        at = device_of(slot) * ROWS
        cot_send[slot] = jnp.concatenate(
            [
                stage_s[pl.ds(pl.multiple_of(row * LENGTH + at, ROWS), ROWS), :]
                for row in range(ROWS)
            ],
            axis=0,
        ).astype(BF16)

    loop(0, DAP, stage_cot, 4)
    cot_recv[me] = cot_send[me]
    pl.semaphore_wait(barrier, DAP - 1)
    near_start(0)

    def cot_start(step):
        block = lax.rem(first_block + BLOCKS - step, BLOCKS)
        loop(
            0,
            8,
            lambda part: swap_start(cot_send, cot_recv, cot_ss, cot_rs, block * 8 + part),
        )

    far_start(0)
    loop(0, 2, cot_start)

    def forward_block(step):
        block = lax.rem(first_block + step, BLOCKS)

        @pl.when(step == 1)
        def _():
            far_forward(0)
            far_take(0)

        spread_bias(0, block)

        def row(index):
            _, soft = weights(0, index, block)
            short = soft.astype(BF16)
            p_s[index, block] = short
            mix(0, index, block, short)

        loop(0, ROWS, row, ROWS)
        mixture = mix_s[0, :, block_rows(block), :].reshape(ROWS * BLOCK, CHANNELS)
        term = dot(mixture, wo_s[0]).reshape(ROWS, BLOCK, CHANNELS)
        middle = rows_s[0, :, block_rows(block), :].astype(F32) + term
        hat, _ = centre(middle.astype(BF16).astype(F32))
        norm_s[1, :, block_rows(block), :] = (hat * gain_ref[1:2, :]).astype(BF16)

        @pl.when(step == BLOCKS - 1)
        def _():
            bias_start(1)
            near_start(1)

        for part in range(8):
            slot = block * 8 + part
            mid_send[slot] = (
                middle[:, part * ROWS : (part + 1) * ROWS, :]
                .reshape(ROWS * ROWS, CHANNELS)
                .astype(BF16)
            )
            swap_start(mid_send, mid_recv, mid_ss, mid_rs, slot)

    loop(0, BLOCKS, forward_block)
    mid_recv[me] = mid_send[me]

    def chunk(block, index):
        return pl.ds(block * (BLOCK * ROWS) + index, BLOCK, stride=ROWS)

    def unpack(recv, block):
        at = pl.ds(pl.multiple_of(block * (BLOCK * ROWS), BLOCK * ROWS), BLOCK * ROWS)
        pieces = recv[pl.ds(pl.multiple_of(block * 8, 8), 8)]
        stage_s[at, :] = pieces.astype(F32).reshape(BLOCK * ROWS, CHANNELS)

    def middle_block(step):
        block = lax.rem(first_block + BLOCKS - step, BLOCKS)
        swap_take(mid_recv, mid_ss, mid_rs, block)
        unpack(mid_recv, block)

        @pl.when(step == 1)
        def _():
            far_start(1)

        def row(index):
            values = stage_s[chunk(block, index), :]
            rows_s[1, index, block_rows(block), :] = values.astype(BF16)
            normalise(1, index, block_rows(block), values)

        loop(0, ROWS, row, ROWS)

    loop(0, BLOCKS, middle_block)
    far_forward(1)
    loop(2, BLOCKS, cot_start)
    project(1)
    far_take(1)
    for head in range(HEADS):
        pieces = bias_all[1].astype(F32)[:, head * ROWS : (head + 1) * ROWS, :]
        bias_two[head] = pieces.reshape(LENGTH, LENGTH).T

    def load_cot(block):
        swap_take(cot_recv, cot_ss, cot_rs, block)
        unpack(cot_recv, block)
        for index in range(ROWS):
            dy_s[1, index, block_rows(block), :] = stage_s[chunk(block, index), :].astype(BF16)

    backward(1, load_cot, lambda step: None)

    def emit_back(block, index, values):
        stage_s[chunk(block, index), :] = values

    def back_start(block):
        for part in range(8):
            slot = block * 8 + part
            at = pl.ds(pl.multiple_of(slot * (ROWS * ROWS), ROWS * ROWS), ROWS * ROWS)
            back_send[slot] = stage_s[at, :].astype(BF16)
            swap_start(back_send, back_recv, back_ss, back_rs, slot)

    input_grads(1, BLOCKS - 1, emit_back, back_start)
    back_recv[me] = back_send[me]

    def load_back(block):
        swap_take(back_recv, back_ss, back_rs, block)
        pieces = [
            back_recv[block * 8 + part].astype(F32).reshape(ROWS, ROWS, CHANNELS)
            for part in range(8)
        ]
        dy_s[0, :, block_rows(block), :] = jnp.concatenate(pieces, axis=1).astype(BF16)

    backward(0, load_back, sum_layer_one)
    wg_start()
    stage_all(3).wait_recv()
    stage_five().start()

    def emit_pair(block, index, values):
        short = values.astype(BF16)
        for z in range(4):
            at = pl.ds(pl.multiple_of(z * 64 + block * 16, 16), 16)
            dpair_ref[index, at, :] = short[z * 16 : z * 16 + 16]

    input_grads(0, 1, emit_pair, lambda block: None)
    small_start(0)
    pair_store.start()
    weight_sums()
    weight_out_one()
    for copy in weight_stores(1):
        copy.start()
    small_out(1)
    small_out(0)
    weight_out()
    for copy in weight_stores(0):
        copy.start()

    swap_sent(cot_send, cot_ss, cot_rs)
    swap_sent(mid_send, mid_ss, mid_rs)
    swap_sent(back_send, back_ss, back_rs)
    bias_sent(0)
    bias_sent(1)
    tiles_all(wg_recv, 0).wait_send()
    tiles_all(wg_recv, 1).wait_send()
    wa_pass().wait_send()

    for index in range(4):
        stage_all(index).wait_send()
    stage_five().wait_send()
    for layer in range(2):
        wg_pair(layer).wait_send()
        small_all(layer).wait_send()

        db_all(layer).wait_send()

        def pair_sent(block):
            remote(
                db_pair_send.at[layer, block],
                db_pair_recv.at[layer, block],
                pair_ss.at[layer, block],
                pair_rs.at[layer, block],
                sibling,
            ).wait_send()

        loop(0, BLOCKS, pair_sent)

    for copy in [pair_store] + weight_stores(1) + weight_stores(0):
        copy.wait()


def finish_kernel(
    pair_ref, small_ref, proj_ref, out_ref, d_pair_ref, ggain_ref, gproj_ref, gbias_ref, gout_ref
):
    d_pair_ref[...] = pair_ref[...]
    gproj_ref[...] = proj_ref[...]
    gout_ref[...] = out_ref[...]
    for layer in range(2):
        gbias_ref[layer] = small_ref[layer, :HEADS, :]
        ggain_ref[layer : layer + 1, :] = small_ref[layer, HEADS : HEADS + 1, :]


def per_device(pair_rep, cotangent, norm_gain, w_project, w_bias, w_out):
    cells = (ROWS, LENGTH, CHANNELS)
    piece = (ROWS * ROWS, CHANNELS)
    bias_piece = (HEADS * ROWS, LENGTH)
    vmem = pltpu.VMEM
    sem = pltpu.SemaphoreType.DMA
    scratch = [
        vmem(cells, BF16),
        vmem(cells, BF16),
        vmem((2, CHANNELS), F32),
        vmem((2, CHANNELS, 4 * CHANNELS), F32),
        vmem((2, HEADS, CHANNELS), F32),
        vmem((2, CHANNELS, CHANNELS), F32),
        vmem(cells, BF16),
        vmem((2, CHANNELS, 4 * CHANNELS), F32),
        vmem((2, CHANNELS, CHANNELS), F32),
        sem((6,)),
        sem((5,)),
        vmem((2,) + cells, BF16),
        vmem((2,) + cells, BF16),
        vmem((2,) + cells, BF16),
        vmem((2,) + cells, BF16),
        vmem((2,) + cells, BF16),
        vmem((2,) + cells, BF16),
        vmem((2,) + cells, F32),
        vmem((2,) + cells, F32),
        vmem((2,) + cells, BF16),
        vmem((ROWS, BLOCKS, STACK, LENGTH), BF16),
        vmem((ROWS, LENGTH, 4 * CHANNELS), BF16),
        vmem((ROWS, CHANNELS, LENGTH), F32),
        vmem((ROWS, CHANNELS, LENGTH), F32),
        vmem((2, CHANNELS, 4 * CHANNELS), BF16),
        vmem((2, CHANNELS, CHANNELS), BF16),
        vmem((2, ROWS, CHANNELS), F32),
        vmem((2, HEADS * ROWS, CHANNELS), F32),
        vmem((2, DAP) + bias_piece, BF16),
        vmem((HEADS, LENGTH, LENGTH), F32),
        vmem((STACK, LENGTH), F32),
        vmem((ROWS, BLOCK, CHANNELS), F32),
        vmem((STACK, LENGTH), F32),
        vmem((CHANNELS, 5 * CHANNELS), F32),
        vmem((ROWS * LENGTH, CHANNELS), F32),
        vmem((DAP,) + piece, BF16),
        vmem((DAP,) + piece, BF16),
        vmem((DAP,) + piece, BF16),
        vmem((DAP,) + piece, BF16),
        vmem((DAP,) + piece, BF16),
        vmem((DAP,) + piece, BF16),
        vmem((BLOCKS, 4) + bias_piece, F32),
        vmem((2, BLOCKS, 4) + bias_piece, BF16),
        vmem((2, BLOCKS, 4) + bias_piece, BF16),
        vmem((2, BLOCKS, 4) + bias_piece, BF16),
        vmem((2, DAP // 2) + bias_piece, BF16),
        vmem((2, HEADS * ROWS, CHANNELS), F32),
        vmem(cells, F32),
        vmem((2, 2, CHANNELS, 3 * CHANNELS), F32),
        vmem((2, CHANNELS, 3 * CHANNELS), F32),
        vmem((2, CHANNELS, 3 * CHANNELS), F32),
        vmem((DAP // 2, ROWS, 3 * CHANNELS), F32),
        vmem((2, DAP // 2, ROWS, 3 * CHANNELS), F32),
        vmem((4, 4 * ROWS, 3 * CHANNELS), F32),
        vmem((4 * ROWS, 3 * CHANNELS), F32),
        vmem((4, ROWS, 3 * CHANNELS), F32),
        vmem((CHANNELS, 3 * CHANNELS), F32),
        vmem((CHANNELS, 3 * CHANNELS), F32),
        vmem((2, DAP, ROWS, CHANNELS), F32),
        sem((1,)),
        sem((BLOCKS,)),
        sem((1,)),
        sem((BLOCKS,)),
        sem((1,)),
        sem((BLOCKS,)),
        sem((2,)),
        sem((2,)),
        sem((2,)),
        sem((2,)),
        sem((2,)),
        sem((2,)),
        sem((2, BLOCKS)),
        sem((2, BLOCKS)),
        sem((2,)),
        sem((2,)),
        sem((3, 2)),
        sem((4,)),
        sem((4,)),
        sem((3,)),
        sem((3,)),
        sem((2,)),
        sem((2,)),
    ]
    whole = pl.BlockSpec(memory_space=pl.ANY)
    held = pl.BlockSpec(memory_space=pltpu.VMEM)
    d_pair, small, grad_project, grad_out = pl.pallas_call(
        kernel,
        out_shape=(
            jax.ShapeDtypeStruct(cells, BF16),
            jax.ShapeDtypeStruct((2, ROWS, CHANNELS), F32),
            jax.ShapeDtypeStruct((2, CHANNELS, 4 * CHANNELS), F32),
            jax.ShapeDtypeStruct((2, CHANNELS, CHANNELS), F32),
        ),
        in_specs=[whole] * 6,
        out_specs=[whole, held, whole, whole],
        scratch_shapes=scratch,
        compiler_params=pltpu.CompilerParams(
            collective_id=0, has_side_effects=True, vmem_limit_bytes=56 << 20
        ),
    )(pair_rep, cotangent, norm_gain, w_project, jnp.swapaxes(w_bias, 1, 2), w_out)
    outputs = pl.pallas_call(
        finish_kernel,
        out_shape=(
            jax.ShapeDtypeStruct(cells, BF16),
            jax.ShapeDtypeStruct((2, CHANNELS), F32),
            jax.ShapeDtypeStruct((2, CHANNELS, 4 * CHANNELS), F32),
            jax.ShapeDtypeStruct((2, HEADS, CHANNELS), F32),
            jax.ShapeDtypeStruct((2, CHANNELS, CHANNELS), F32),
        ),
        in_specs=[pl.BlockSpec(memory_space=pltpu.VMEM)] * 4,
        out_specs=[pl.BlockSpec(memory_space=pltpu.VMEM)] * 5,
    )(d_pair, small, grad_project, grad_out)
    return outputs[:3] + (jnp.swapaxes(outputs[3], 1, 2), outputs[4])


def solution(mesh):
    in_specs = (P(("dp", "dap"), None, None), P(("dp", "dap"), None, None), P(), P(), P(), P())
    out_specs = (
        P(("dp", "dap"), None, None),
        P("dp", None),
        P("dp", None, None),
        P("dp", None, None),
        P("dp", None, None),
    )
    return jax.shard_map(
        per_device, mesh=mesh, in_specs=in_specs, out_specs=out_specs, check_vma=False
    )
```

```python
import jax
import jax.numpy as jnp
from jax import lax
from jax.experimental import pallas as pl
from jax.experimental.pallas import tpu as pltpu
from jax.sharding import PartitionSpec as P

EPS = 1e-05
MESH = pl.DeviceIdType.MESH
F32 = jnp.float32
BF16 = jnp.bfloat16
DAP = 32
ROWS = 8
LENGTH = 256
CHANNELS = 128
HEADS = 4
BLOCKS = 4
BLOCK = LENGTH // BLOCKS
STACK = HEADS * BLOCK
SCALE = (CHANNELS // HEADS) ** (-0.5)


def slot_of(device):
    return (
        lax.rem(lax.div(device, 2), 4) * 8 + lax.div(device, 8) * 2 + lax.rem(device, 2)
    )


def device_of(slot):
    return lax.rem(lax.div(slot, 2), 4) * 8 + lax.div(slot, 8) * 2 + lax.rem(slot, 2)


def remote(src, dst, send_sem, recv_sem, slot):
    return pltpu.make_async_remote_copy(
        src_ref=src,
        dst_ref=dst,
        send_sem=send_sem,
        recv_sem=recv_sem,
        device_id=(lax.axis_index("dp"), device_of(slot)),
        device_id_type=MESH,
    )


def loop(low, high, body, unroll=1):
    def step(index, carry):
        body(index)
        return carry

    lax.fori_loop(low, high, step, 0, unroll=unroll)


def dot(a, b):
    return lax.dot_general(a, b, (((1,), (0,)), ((), ())), preferred_element_type=F32)


def dot_nt(a, b):
    return lax.dot_general(a, b, (((1,), (1,)), ((), ())), preferred_element_type=F32)


def dot_tn(a, b):
    return lax.dot_general(a, b, (((0,), (0,)), ((), ())), preferred_element_type=F32)


def centre(values):
    centred = values - jnp.mean(values, axis=-1, keepdims=True)
    variance = jnp.mean(centred * centred, axis=-1, keepdims=True)
    inverse = lax.rsqrt(variance + EPS)
    return centred * inverse, inverse


def kernel(
    x_hbm,
    cot_hbm,
    gain_hbm,
    wp_hbm,
    wb_hbm,
    wo_hbm,
    dpair_hbm,
    small_ref,
    gproj_hbm,
    gout_hbm,
    x_ref,
    cot_ref,
    gain_ref,
    wp_ref,
    wb_ref,
    wo_ref,
    dpair_ref,
    gproj_ref,
    gout_ref,
    in_s,
    out_s,
    rows_s,
    dy_s,
    norm_s,
    q_s,
    k_s,
    v_s,
    gate_s,
    o_s,
    mix_s,
    p_s,
    scores_s,
    dproj_s,
    dkt_s,
    dvt_s,
    wp_s,
    wo_s,
    wb_s,
    bias_f,
    bias_all,
    bias_two,
    bias_q,
    dm_s,
    dbias_acc,
    wide_s,
    stage_s,
    cot_send,
    cot_recv,
    mid_send,
    mid_recv,
    back_send,
    back_recv,
    db_kept,
    db_pair_send,
    db_pair_recv,
    db_send,
    db_recv,
    db_s,
    dn_s,
    wg_half,
    wg_held,
    wg_tot,
    wg_recv,
    wg_all,
    wy_recv,
    wy_tot,
    wz_recv,
    wg_own,
    wg_other,
    sg_all,
    cot_ss,
    cot_rs,
    mid_ss,
    mid_rs,
    back_ss,
    back_rs,
    bias_ss,
    bias_rs,
    far_ss,
    far_rs,
    pass_ss,
    pass_rs,
    pair_ss,
    pair_rs,
    db_ss,
    db_rs,
    wg_ps,
    st_ss,
    st_rs,
    wg_ss,
    wg_rs,
    sg_ss,
    sg_rs,
):
    me = slot_of(lax.axis_index("dap"))
    mine = lax.div(me, 2)
    core = lax.rem(me, 2)
    sibling = me + 1 - 2 * core
    first_block = lax.div(me, 8)
    barrier = pltpu.get_barrier_semaphore()

    def other(step):
        return lax.rem(me + step, DAP)

    def tell(step):
        pl.semaphore_signal(
            barrier,
            inc=1,
            device_id=(lax.axis_index("dp"), device_of(other(step))),
            device_id_type=MESH,
        )

    loop(1, DAP, tell, 31)

    def load(src, dst, index):
        return pltpu.make_async_copy(src, dst, in_s.at[index])

    x_load = load(x_hbm, x_ref, 0)
    gain_load = load(gain_hbm, gain_ref, 1)
    wb_load = load(wb_hbm, wb_ref, 2)
    weight_loads = [load(wp_hbm, wp_ref, 3), load(wo_hbm, wo_ref, 4)]
    cot_load = load(cot_hbm, cot_ref, 5)
    for copy in [gain_load, wb_load, x_load] + weight_loads + [cot_load]:
        copy.start()

    def store(src, dst, index):
        return pltpu.make_async_copy(src, dst, out_s.at[index])

    pair_store = store(dpair_ref, dpair_hbm, 0)

    def weight_stores(layer):
        return [
            store(gproj_ref.at[layer], gproj_hbm.at[layer], 1 + layer),
            store(gout_ref.at[layer], gout_hbm.at[layer], 3 + layer),
        ]

    lane_head = lax.div(lax.broadcasted_iota(jnp.int32, (1, CHANNELS), 1), CHANNELS // HEADS)
    masks = [jnp.where(lane_head == head, 1.0, 0.0).astype(F32) for head in range(HEADS)]
    masks_short = [mask.astype(BF16) for mask in masks]

    def stack(block):
        return jnp.concatenate([block * mask for mask in masks_short], axis=0)

    def pick(stacked):
        out = stacked[:BLOCK] * masks[0]
        for head in range(1, HEADS):
            out = out + stacked[head * BLOCK : (head + 1) * BLOCK] * masks[head]
        return out

    def block_rows(block):
        return pl.ds(pl.multiple_of(block * BLOCK, BLOCK), BLOCK)

    def along_y(y):
        return y * 8 + lax.rem(me, 8)

    def turn(at, step):
        return lax.rem(at + step, 4)

    def near(step):
        return first_block * 8 + lax.rem(lax.rem(me, 8) + step, 8)

    def near_copy(layer, slot):
        return remote(
            bias_all.at[layer, me], bias_all.at[layer, me], bias_ss.at[layer], bias_rs.at[layer], slot
        )

    def near_all(layer):
        held = bias_all.at[layer, pl.ds(0, 7)]
        return remote(held, held, bias_ss.at[layer], bias_rs.at[layer], sibling)

    def far_all(layer, ss, rs):
        held = bias_all.at[layer, pl.ds(0, 12)]
        return remote(held, held, ss.at[layer], rs.at[layer], sibling)

    def half_of(y, half):
        return pl.ds(pl.multiple_of(y * 8 + half * 4, 4), 4)

    def far_copy(layer, y):
        held = bias_all.at[layer, half_of(first_block, core)]
        return remote(held, held, far_ss.at[layer], far_rs.at[layer], along_y(y))

    def far_pass(layer, y):
        held = bias_all.at[layer, half_of(y, core)]
        return remote(held, held, pass_ss.at[layer], pass_rs.at[layer], sibling)

    def near_start(layer):
        loop(1, 8, lambda step: near_copy(layer, near(step)).start(), 7)

    def far_start(layer):
        near_all(layer).wait_recv()
        loop(1, 4, lambda step: far_copy(layer, turn(first_block, step)).start(), 3)

    def far_forward(layer):
        far_all(layer, far_ss, far_rs).wait_recv()
        loop(1, 4, lambda step: far_pass(layer, turn(first_block, step)).start(), 3)

    def far_take(layer):
        far_all(layer, pass_ss, pass_rs).wait_recv()

    def bias_sent(layer):
        near_all(layer).wait_send()
        far_all(layer, far_ss, far_rs).wait_send()
        far_all(layer, pass_ss, pass_rs).wait_send()

    def swap_start(send, recv, ss, rs, slot):
        @pl.when(slot != me)
        def _():
            remote(send.at[slot], recv.at[me], ss.at[0], rs.at[first_block], slot).start()

    def swap_take(recv, ss, rs, block):
        def take(count):
            held = recv.at[pl.ds(0, count)]
            remote(held, held, ss.at[0], rs.at[block], sibling).wait_recv()

        @pl.when(block == first_block)
        def _():
            take(7)

        @pl.when(block != first_block)
        def _():
            take(8)

    def swap_sent(send, ss, rs):
        held = send.at[pl.ds(0, DAP - 1)]
        remote(held, held, ss.at[0], rs.at[0], sibling).wait_send()

    def normalise(layer, index, at, values):
        hat, _ = centre(values)
        norm_s[layer, index, at, :] = (hat * gain_ref[layer : layer + 1, :]).astype(BF16)

    def bias_start(layer):
        weight = wb_s[layer].astype(BF16)

        def row(index):
            bias = dot_nt(weight, norm_s[layer, index])
            for half in range(2):
                bias_f[half, pl.ds(index, HEADS, stride=ROWS), :] = bias[
                    :HEADS, half * CHANNELS : (half + 1) * CHANNELS
                ]

        loop(0, ROWS, row, ROWS)
        bias_all[layer, me] = jnp.concatenate([bias_f[0], bias_f[1]], axis=1).astype(BF16)

    def project(layer):
        def row(index):
            projected = dot(norm_s[layer, index], wp_s[layer])
            q_s[layer, index] = (projected[:, :CHANNELS] * SCALE).astype(BF16)
            k_s[layer, index] = projected[:, CHANNELS : 2 * CHANNELS].astype(BF16)
            v_s[layer, index] = projected[:, 2 * CHANNELS : 3 * CHANNELS].astype(BF16)
            gate_s[layer, index] = 1.0 / (1.0 + jnp.exp(-projected[:, 3 * CHANNELS :]))

        loop(0, ROWS, row, ROWS)

    def spread_bias(layer, block):
        if layer == 1:
            for head in range(HEADS):
                at = head * BLOCK
                bias_q[at : at + BLOCK, :] = bias_two[head, block_rows(block), :]
            return
        for part in range(8):
            piece = bias_all[layer, block * 8 + part].astype(F32)
            for head in range(HEADS):
                at = head * BLOCK + part * ROWS
                bias_q[at : at + ROWS, :] = piece[head * ROWS : (head + 1) * ROWS]

    def products(layer):
        def one_block(block):
            def row(index):
                queries = stack(q_s[layer, index, block_rows(block), :])
                scores_s[index, block] = dot_nt(queries, k_s[layer, index])

            loop(0, ROWS, row, ROWS)

        loop(0, BLOCKS, one_block)

    def weights(layer, index, block):
        queries = stack(q_s[layer, index, block_rows(block), :])
        scores = scores_s[index, block] + bias_q[...]
        shifted = jnp.exp(scores - jnp.max(scores, axis=-1, keepdims=True))
        return queries, shifted * (1.0 / jnp.sum(shifted, axis=-1, keepdims=True))

    def mix(layer, index, block, short):
        mixed = pick(dot(short, v_s[layer, index]))
        o_s[layer, index, block_rows(block), :] = mixed
        gate = gate_s[layer, index, block_rows(block), :]
        mix_s[layer, index, block_rows(block), :] = (mixed * gate).astype(BF16)
        return mixed

    def backward(layer, load_dy, between):
        dkt_s[...] = jnp.zeros(dkt_s.shape, F32)
        dvt_s[...] = jnp.zeros(dvt_s.shape, F32)

        def pass_on(block):
            remote(
                db_pair_send.at[layer, block],
                db_pair_recv.at[layer, block],
                pair_ss.at[layer, block],
                pair_rs.at[layer, block],
                sibling,
            ).wait_recv()
            for z in range(4):
                total = db_kept[block, z] + db_pair_recv[layer, block, z].astype(F32)
                db_send[layer, block, z] = total.astype(BF16)
                slot = block * 8 + z * 2 + core

                @pl.when(slot != me)
                def _():
                    remote(
                        db_send.at[layer, block, z],
                        db_recv.at[layer, mine],
                        db_ss.at[layer],
                        db_rs.at[layer],
                        slot,
                    ).start()

                @pl.when(slot == me)
                def _():
                    db_recv[layer, mine] = db_send[layer, block, z]

        def step_block(step):
            block = lax.rem(first_block + step, BLOCKS)
            load_dy(block)
            between(step)
            dy = dy_s[layer, :, block_rows(block), :].reshape(ROWS * BLOCK, CHANNELS)
            dm_s[...] = dot_nt(dy, wo_s[layer]).astype(BF16).astype(F32).reshape(dm_s.shape)
            spread_bias(layer, block)
            dbias_acc[...] = jnp.zeros(dbias_acc.shape, F32)

            def row(index):
                at = block_rows(block)
                if layer == 0:
                    queries = stack(q_s[layer, index, at, :])
                    short = p_s[index, block]
                    soft = short.astype(F32)
                    mixed = o_s[layer, index, at, :]
                else:
                    queries, soft = weights(layer, index, block)
                    short = soft.astype(BF16)
                    mixed = mix(layer, index, block, short)
                gate = gate_s[layer, index, at, :]
                dm = dm_s[index]
                d_gate = dm * mixed * gate * (1.0 - gate)
                dproj_s[index, at, 3 * CHANNELS :] = d_gate.astype(BF16)
                d_mixed = stack((dm * gate).astype(BF16))
                d_soft = dot_nt(d_mixed, v_s[layer, index]).astype(BF16).astype(F32)
                product = soft * d_soft
                d_scores = product - soft * jnp.sum(product, axis=-1, keepdims=True)
                dbias_acc[...] += d_scores
                d_short = d_scores.astype(BF16)
                d_query = pick(dot(d_short, k_s[layer, index])).astype(BF16).astype(F32)
                dproj_s[index, at, :CHANNELS] = (d_query * SCALE).astype(BF16)
                dkt_s[index] += dot_tn(queries, d_short)
                dvt_s[index] += dot_tn(d_mixed, short)

            loop(0, ROWS, row, ROWS)
            for z in range(4):
                for half in range(2):
                    part = z * 2 + half
                    piece = jnp.concatenate(
                        [
                            dbias_acc[
                                head * BLOCK + part * ROWS : head * BLOCK + (part + 1) * ROWS, :
                            ]
                            for head in range(HEADS)
                        ],
                        axis=0,
                    )

                    @pl.when(core == half)
                    def _():
                        db_kept[block, z] = piece

                    @pl.when(core != half)
                    def _():
                        db_pair_send[layer, block, z] = piece.astype(BF16)

            remote(
                db_pair_send.at[layer, block],
                db_pair_recv.at[layer, block],
                pair_ss.at[layer, block],
                pair_rs.at[layer, block],
                sibling,
            ).start()

            @pl.when(step > 0)
            def _():
                pass_on(lax.rem(first_block + step + BLOCKS - 1, BLOCKS))

        loop(0, BLOCKS, step_block)
        wide_s[...] = jnp.zeros(wide_s.shape, F32)

        def row_grads(index):
            dproj_s[index, :, CHANNELS : 2 * CHANNELS] = dkt_s[index].T.astype(BF16)
            dproj_s[index, :, 2 * CHANNELS : 3 * CHANNELS] = dvt_s[index].T.astype(BF16)
            wide_s[:, : 4 * CHANNELS] += dot_tn(norm_s[layer, index], dproj_s[index])
            wide_s[:, 4 * CHANNELS :] += dot_tn(mix_s[layer, index], dy_s[layer, index])

        loop(0, ROWS, row_grads, ROWS)
        pass_on(lax.rem(first_block + BLOCKS - 1, BLOCKS))
        for half in range(2):
            at = half * 2 * CHANNELS
            wg_half[layer, half, :, : 2 * CHANNELS] = wide_s[:, at : at + 2 * CHANNELS]
            wg_half[layer, half, :, 2 * CHANNELS :] = wide_s[:, 4 * CHANNELS :]
        wg_pair(layer).start()

        def main(index):
            dn_s[index] = dot_nt(dproj_s[index], wp_s[layer])

        loop(0, ROWS, main, ROWS)

    def wg_pair(layer):
        return remote(
            wg_half.at[layer, 1 - core],
            wg_held.at[layer],
            wg_ps.at[layer, 0],
            wg_ps.at[layer, 1],
            sibling,
        )

    def wg_add(layer):
        wg_pair(layer).wait_recv()
        wg_tot[layer] = wg_half[layer, core] + wg_held[layer]

    def tile(slot):
        return pl.ds(pl.multiple_of(lax.div(slot, 2) * ROWS, ROWS), ROWS)

    def wg_copy(slot):
        return remote(
            wg_tot.at[0, tile(slot), :], wg_recv.at[mine], wg_ss.at[0], wg_rs.at[0], slot
        )

    def tiles_all(held, index):
        piece = held.at[pl.ds(0, DAP // 2 - 1)]
        return remote(piece, piece, wg_ss.at[index], wg_rs.at[index], sibling)

    def wa_copy(slot):
        held = wg_all.at[core, mine]
        return remote(held, held, wg_ss.at[1], wg_rs.at[1], slot)

    def wa_pass():
        return remote(wg_all.at[core], wg_all.at[core], wg_ss.at[2], wg_rs.at[2], sibling)

    def wg_start():
        wg_add(0)
        loop(1, DAP // 2, lambda step: wg_copy(other(2 * step)).start(), 5)
        wg_recv[mine] = wg_tot[0, tile(me), :]

    my_z = lax.rem(mine, 4)

    def along_z(z):
        return first_block * 8 + z * 2 + core

    def quarter(y):
        return pl.ds(pl.multiple_of(y * 32, 32), 32)

    def eighth(y, z):
        return pl.ds(pl.multiple_of(y * 32 + z * 8, 8), 8)

    def stage_one(y):
        return remote(
            wg_tot.at[1, quarter(y), :],
            wy_recv.at[first_block],
            st_ss.at[0],
            st_rs.at[0],
            along_y(y),
        )

    def stage_two(z):
        return remote(
            wy_tot.at[pl.ds(pl.multiple_of(z * 8, 8), 8), :],
            wz_recv.at[my_z],
            st_ss.at[1],
            st_rs.at[1],
            along_z(z),
        )

    def stage_three(z):
        held = wg_own.at[eighth(first_block, my_z), :]
        return remote(held, held, st_ss.at[2], st_rs.at[2], along_z(z))

    def stage_four(y):
        held = wg_own.at[quarter(first_block), :]
        return remote(held, held, st_ss.at[3], st_rs.at[3], along_y(y))

    def stage_all(index):
        rows = (3 * 32, 3 * 8, 3 * 8, 3 * 32)[index]
        held = wg_own.at[pl.ds(0, rows), :]
        return remote(held, held, st_ss.at[index], st_rs.at[index], sibling)

    def stage_five():
        return remote(wg_own, wg_other, wg_ps.at[2, 0], wg_ps.at[2, 1], sibling)

    def three(copy, at):
        loop(1, 4, lambda step: copy(turn(at, step)).start())

    def sum_layer_one(step):
        @pl.when(step == 0)
        def _():
            wg_add(1)
            three(stage_one, first_block)
            wy_recv[first_block] = wg_tot[1, quarter(first_block), :]

        @pl.when(step == 1)
        def _():
            stage_all(0).wait_recv()
            wy_tot[...] = wy_recv[0] + wy_recv[1] + wy_recv[2] + wy_recv[3]
            three(stage_two, my_z)
            wz_recv[my_z] = wy_tot[pl.ds(pl.multiple_of(my_z * 8, 8), 8), :]
            small_start(1)

        @pl.when(step == 2)
        def _():
            stage_all(1).wait_recv()
            wg_own[eighth(first_block, my_z), :] = (
                wz_recv[0] + wz_recv[1] + wz_recv[2] + wz_recv[3]
            )
            three(stage_three, my_z)

        @pl.when(step == 3)
        def _():
            stage_all(2).wait_recv()
            three(stage_four, first_block)

    def db_all(layer):
        held = db_recv.at[layer, pl.ds(0, DAP // 2 - 1)]
        return remote(held, held, db_ss.at[layer], db_rs.at[layer], sibling)

    def finish_bias(layer):
        db_all(layer).wait_recv()
        total = lax.fori_loop(
            0,
            DAP // 2,
            lambda chip, total: total + db_recv[layer, chip].astype(F32),
            jnp.zeros((HEADS * ROWS, LENGTH), F32),
        )
        for half in range(2):
            db_s[half] = (
                total[:, half * CHANNELS : (half + 1) * CHANNELS].astype(BF16).astype(F32)
            )

    def input_grads(layer, direction, emit, emitted):
        finish_bias(layer)
        zero = jnp.zeros((ROWS, CHANNELS), F32)
        weight = wb_s[layer].astype(BF16)
        gain = gain_ref[layer : layer + 1, :]

        def add_bias(index, total):
            at = pl.ds(index, HEADS, stride=ROWS)
            rows = jnp.concatenate([db_s[0, at, :], db_s[1, at, :]], axis=1)
            rows = jnp.concatenate([rows, jnp.zeros((ROWS - HEADS, LENGTH), F32)], axis=0)
            rows = rows.astype(BF16)
            dn_s[index] += dot_tn(rows, weight)
            return total + dot(rows, norm_s[layer, index])

        grad_bias = lax.fori_loop(0, ROWS, add_bias, zero, unroll=ROWS)

        def step_block(step, total):
            block = lax.rem(first_block + direction * step, BLOCKS)
            at = block_rows(block)

            def row(index, total):
                d_normed = dn_s[index, at, :]
                hat, inverse = centre(rows_s[layer, index, at, :].astype(F32))
                d_hat = d_normed * gain
                d_input = inverse * (
                    d_hat
                    - jnp.mean(d_hat, axis=-1, keepdims=True)
                    - hat * jnp.mean(d_hat * hat, axis=-1, keepdims=True)
                )
                emit(block, index, dy_s[layer, index, at, :].astype(F32) + d_input)
                return total + jnp.sum(d_normed * hat, axis=0, keepdims=True)

            total = lax.fori_loop(0, ROWS, row, total, unroll=ROWS)
            emitted(block)
            return total

        grad_gain = lax.fori_loop(0, BLOCKS, step_block, jnp.zeros((1, CHANNELS), F32))
        sg_all[layer, me] = jnp.concatenate(
            [grad_bias[:HEADS], grad_gain, zero[: ROWS - HEADS - 1]], axis=0
        )

    def small_copy(layer, slot):
        held = sg_all.at[layer, me]
        return remote(held, held, sg_ss.at[layer], sg_rs.at[layer], slot)

    def small_all(layer):
        held = sg_all.at[layer, pl.ds(0, DAP - 1)]
        return remote(held, held, sg_ss.at[layer], sg_rs.at[layer], sibling)

    def small_start(layer):
        loop(1, DAP, lambda step: small_copy(layer, other(step)).start(), 31)

    def weight_sums():
        tiles_all(wg_recv, 0).wait_recv()
        total = wg_recv[0]
        for chip in range(1, DAP // 2):
            total = total + wg_recv[chip]
        wg_all[core, mine] = total
        loop(1, DAP // 2, lambda step: wa_copy(other(2 * step)).start(), 5)

    def small_out(layer):
        small_all(layer).wait_recv()
        total = sg_all[layer, 0]
        for slot in range(1, DAP):
            total = total + sg_all[layer, slot]
        small_ref[layer] = total

    def weight_out():
        tiles_all(wg_all.at[core], 1).wait_recv()
        wa_pass().start()
        wa_pass().wait_recv()

        def place(chip):
            at = pl.ds(pl.multiple_of(chip * 8, 8), 8)
            gproj_ref[0, at, : 2 * CHANNELS] = wg_all[0, chip, :, : 2 * CHANNELS]
            gproj_ref[0, at, 2 * CHANNELS :] = wg_all[1, chip, :, : 2 * CHANNELS]
            gout_ref[0, at, :] = wg_all[0, chip, :, 2 * CHANNELS :]

        loop(0, DAP // 2, place, 4)

    def weight_out_one():
        stage_five().wait_recv()
        gout_ref[1] = wg_own[:, 2 * CHANNELS :]

        @pl.when(core == 0)
        def _():
            gproj_ref[1, :, : 2 * CHANNELS] = wg_own[:, : 2 * CHANNELS]
            gproj_ref[1, :, 2 * CHANNELS :] = wg_other[:, : 2 * CHANNELS]

        @pl.when(core == 1)
        def _():
            gproj_ref[1, :, : 2 * CHANNELS] = wg_other[:, : 2 * CHANNELS]
            gproj_ref[1, :, 2 * CHANNELS :] = wg_own[:, : 2 * CHANNELS]

    for copy in [gain_load, wb_load, x_load]:
        copy.wait()
    for layer in range(2):
        wb_s[layer] = jnp.concatenate(
            [wb_ref[layer], jnp.zeros((ROWS - HEADS, CHANNELS), F32)], axis=0
        )
    for y in range(4):
        for z in range(4):
            rows_s[0, :, y * 64 + z * 16 : y * 64 + z * 16 + 16, :] = x_ref[
                :, z * 64 + y * 16 : z * 64 + y * 16 + 16, :
            ]
    whole = pl.ds(0, LENGTH)
    loop(0, ROWS, lambda index: normalise(0, index, whole, rows_s[0, index].astype(F32)), ROWS)
    bias_start(0)
    for copy in weight_loads:
        copy.wait()
    for layer in range(2):
        wp_s[layer] = wp_ref[layer].astype(BF16)
        wo_s[layer] = wo_ref[layer].astype(BF16)
    project(0)
    cot_load.wait()
    stage_s[...] = cot_ref[...].astype(F32).reshape(stage_s.shape)

    def stage_cot(slot):
        at = device_of(slot) * ROWS
        cot_send[slot] = jnp.concatenate(
            [
                stage_s[pl.ds(pl.multiple_of(row * LENGTH + at, ROWS), ROWS), :]
                for row in range(ROWS)
            ],
            axis=0,
        ).astype(BF16)

    loop(0, DAP, stage_cot, 4)
    cot_recv[me] = cot_send[me]
    pl.semaphore_wait(barrier, DAP - 1)
    near_start(0)
    products(0)

    def cot_start(step):
        block = lax.rem(first_block + BLOCKS - step, BLOCKS)
        loop(
            0,
            8,
            lambda part: swap_start(cot_send, cot_recv, cot_ss, cot_rs, block * 8 + part),
            8,
        )

    far_start(0)
    loop(0, 2, cot_start)

    def forward_block(step):
        block = lax.rem(first_block + step, BLOCKS)

        @pl.when(step == 1)
        def _():
            far_forward(0)
            far_take(0)

        spread_bias(0, block)

        def row(index):
            _, soft = weights(0, index, block)
            short = soft.astype(BF16)
            p_s[index, block] = short
            mix(0, index, block, short)

        loop(0, ROWS, row, ROWS)
        mixture = mix_s[0, :, block_rows(block), :].reshape(ROWS * BLOCK, CHANNELS)
        term = dot(mixture, wo_s[0]).reshape(ROWS, BLOCK, CHANNELS)
        middle = rows_s[0, :, block_rows(block), :].astype(F32) + term
        hat, _ = centre(middle.astype(BF16).astype(F32))
        norm_s[1, :, block_rows(block), :] = (hat * gain_ref[1:2, :]).astype(BF16)

        @pl.when(step == BLOCKS - 1)
        def _():
            bias_start(1)
            near_start(1)

        for part in range(8):
            slot = block * 8 + part
            mid_send[slot] = (
                middle[:, part * ROWS : (part + 1) * ROWS, :]
                .reshape(ROWS * ROWS, CHANNELS)
                .astype(BF16)
            )
            swap_start(mid_send, mid_recv, mid_ss, mid_rs, slot)

    loop(0, BLOCKS, forward_block)
    mid_recv[me] = mid_send[me]

    def chunk(block, index):
        return pl.ds(block * (BLOCK * ROWS) + index, BLOCK, stride=ROWS)

    def unpack(recv, block):
        at = pl.ds(pl.multiple_of(block * (BLOCK * ROWS), BLOCK * ROWS), BLOCK * ROWS)
        pieces = recv[pl.ds(pl.multiple_of(block * 8, 8), 8)]
        stage_s[at, :] = pieces.astype(F32).reshape(BLOCK * ROWS, CHANNELS)

    def middle_block(step):
        block = lax.rem(first_block + BLOCKS - step, BLOCKS)
        swap_take(mid_recv, mid_ss, mid_rs, block)
        unpack(mid_recv, block)

        @pl.when(step == 1)
        def _():
            far_start(1)

        def row(index):
            values = stage_s[chunk(block, index), :]
            rows_s[1, index, block_rows(block), :] = values.astype(BF16)
            normalise(1, index, block_rows(block), values)

        loop(0, ROWS, row, ROWS)

    loop(0, BLOCKS, middle_block)
    far_forward(1)
    loop(2, BLOCKS, cot_start)
    project(1)
    products(1)
    far_take(1)
    for head in range(HEADS):
        pieces = bias_all[1].astype(F32)[:, head * ROWS : (head + 1) * ROWS, :]
        bias_two[head] = pieces.reshape(LENGTH, LENGTH).T

    def load_cot(block):
        swap_take(cot_recv, cot_ss, cot_rs, block)
        unpack(cot_recv, block)
        for index in range(ROWS):
            dy_s[1, index, block_rows(block), :] = stage_s[chunk(block, index), :].astype(BF16)

    backward(1, load_cot, lambda step: None)

    def emit_back(block, index, values):
        stage_s[chunk(block, index), :] = values

    def back_start(block):
        for part in range(8):
            slot = block * 8 + part
            at = pl.ds(pl.multiple_of(slot * (ROWS * ROWS), ROWS * ROWS), ROWS * ROWS)
            back_send[slot] = stage_s[at, :].astype(BF16)
            swap_start(back_send, back_recv, back_ss, back_rs, slot)

    input_grads(1, BLOCKS - 1, emit_back, back_start)
    back_recv[me] = back_send[me]

    def load_back(block):
        swap_take(back_recv, back_ss, back_rs, block)
        pieces = [
            back_recv[block * 8 + part].astype(F32).reshape(ROWS, ROWS, CHANNELS)
            for part in range(8)
        ]
        dy_s[0, :, block_rows(block), :] = jnp.concatenate(pieces, axis=1).astype(BF16)

    backward(0, load_back, sum_layer_one)
    wg_start()
    stage_all(3).wait_recv()
    stage_five().start()

    def emit_pair(block, index, values):
        short = values.astype(BF16)
        for z in range(4):
            at = pl.ds(pl.multiple_of(z * 64 + block * 16, 16), 16)
            dpair_ref[index, at, :] = short[z * 16 : z * 16 + 16]

    input_grads(0, 1, emit_pair, lambda block: None)
    small_start(0)
    pair_store.start()
    weight_sums()
    weight_out_one()
    for copy in weight_stores(1):
        copy.start()
    small_out(1)
    small_out(0)
    weight_out()
    for copy in weight_stores(0):
        copy.start()

    swap_sent(cot_send, cot_ss, cot_rs)
    swap_sent(mid_send, mid_ss, mid_rs)
    swap_sent(back_send, back_ss, back_rs)
    bias_sent(0)
    bias_sent(1)
    tiles_all(wg_recv, 0).wait_send()
    tiles_all(wg_recv, 1).wait_send()
    wa_pass().wait_send()

    for index in range(4):
        stage_all(index).wait_send()
    stage_five().wait_send()
    for layer in range(2):
        wg_pair(layer).wait_send()
        small_all(layer).wait_send()

        db_all(layer).wait_send()

        def pair_sent(block):
            remote(
                db_pair_send.at[layer, block],
                db_pair_recv.at[layer, block],
                pair_ss.at[layer, block],
                pair_rs.at[layer, block],
                sibling,
            ).wait_send()

        loop(0, BLOCKS, pair_sent)

    for copy in [pair_store] + weight_stores(1) + weight_stores(0):
        copy.wait()


def finish_kernel(
    pair_ref, small_ref, proj_ref, out_ref, d_pair_ref, ggain_ref, gproj_ref, gbias_ref, gout_ref
):
    d_pair_ref[...] = pair_ref[...]
    gproj_ref[...] = proj_ref[...]
    gout_ref[...] = out_ref[...]
    for layer in range(2):
        gbias_ref[layer] = small_ref[layer, :HEADS, :]
        ggain_ref[layer : layer + 1, :] = small_ref[layer, HEADS : HEADS + 1, :]


def per_device(pair_rep, cotangent, norm_gain, w_project, w_bias, w_out):
    cells = (ROWS, LENGTH, CHANNELS)
    piece = (ROWS * ROWS, CHANNELS)
    bias_piece = (HEADS * ROWS, LENGTH)
    vmem = pltpu.VMEM
    sem = pltpu.SemaphoreType.DMA
    scratch = [
        vmem(cells, BF16),
        vmem(cells, BF16),
        vmem((2, CHANNELS), F32),
        vmem((2, CHANNELS, 4 * CHANNELS), F32),
        vmem((2, HEADS, CHANNELS), F32),
        vmem((2, CHANNELS, CHANNELS), F32),
        vmem(cells, BF16),
        vmem((2, CHANNELS, 4 * CHANNELS), F32),
        vmem((2, CHANNELS, CHANNELS), F32),
        sem((6,)),
        sem((5,)),
        vmem((2,) + cells, BF16),
        vmem((2,) + cells, BF16),
        vmem((2,) + cells, BF16),
        vmem((2,) + cells, BF16),
        vmem((2,) + cells, BF16),
        vmem((2,) + cells, BF16),
        vmem((2,) + cells, F32),
        vmem((2,) + cells, F32),
        vmem((2,) + cells, BF16),
        vmem((ROWS, BLOCKS, STACK, LENGTH), BF16),
        vmem((ROWS, BLOCKS, STACK, LENGTH), F32),
        vmem((ROWS, LENGTH, 4 * CHANNELS), BF16),
        vmem((ROWS, CHANNELS, LENGTH), F32),
        vmem((ROWS, CHANNELS, LENGTH), F32),
        vmem((2, CHANNELS, 4 * CHANNELS), BF16),
        vmem((2, CHANNELS, CHANNELS), BF16),
        vmem((2, ROWS, CHANNELS), F32),
        vmem((2, HEADS * ROWS, CHANNELS), F32),
        vmem((2, DAP) + bias_piece, BF16),
        vmem((HEADS, LENGTH, LENGTH), F32),
        vmem((STACK, LENGTH), F32),
        vmem((ROWS, BLOCK, CHANNELS), F32),
        vmem((STACK, LENGTH), F32),
        vmem((CHANNELS, 5 * CHANNELS), F32),
        vmem((ROWS * LENGTH, CHANNELS), F32),
        vmem((DAP,) + piece, BF16),
        vmem((DAP,) + piece, BF16),
        vmem((DAP,) + piece, BF16),
        vmem((DAP,) + piece, BF16),
        vmem((DAP,) + piece, BF16),
        vmem((DAP,) + piece, BF16),
        vmem((BLOCKS, 4) + bias_piece, F32),
        vmem((2, BLOCKS, 4) + bias_piece, BF16),
        vmem((2, BLOCKS, 4) + bias_piece, BF16),
        vmem((2, BLOCKS, 4) + bias_piece, BF16),
        vmem((2, DAP // 2) + bias_piece, BF16),
        vmem((2, HEADS * ROWS, CHANNELS), F32),
        vmem(cells, F32),
        vmem((2, 2, CHANNELS, 3 * CHANNELS), F32),
        vmem((2, CHANNELS, 3 * CHANNELS), F32),
        vmem((2, CHANNELS, 3 * CHANNELS), F32),
        vmem((DAP // 2, ROWS, 3 * CHANNELS), F32),
        vmem((2, DAP // 2, ROWS, 3 * CHANNELS), F32),
        vmem((4, 4 * ROWS, 3 * CHANNELS), F32),
        vmem((4 * ROWS, 3 * CHANNELS), F32),
        vmem((4, ROWS, 3 * CHANNELS), F32),
        vmem((CHANNELS, 3 * CHANNELS), F32),
        vmem((CHANNELS, 3 * CHANNELS), F32),
        vmem((2, DAP, ROWS, CHANNELS), F32),
        sem((1,)),
        sem((BLOCKS,)),
        sem((1,)),
        sem((BLOCKS,)),
        sem((1,)),
        sem((BLOCKS,)),
        sem((2,)),
        sem((2,)),
        sem((2,)),
        sem((2,)),
        sem((2,)),
        sem((2,)),
        sem((2, BLOCKS)),
        sem((2, BLOCKS)),
        sem((2,)),
        sem((2,)),
        sem((3, 2)),
        sem((4,)),
        sem((4,)),
        sem((3,)),
        sem((3,)),
        sem((2,)),
        sem((2,)),
    ]
    whole = pl.BlockSpec(memory_space=pl.ANY)
    held = pl.BlockSpec(memory_space=pltpu.VMEM)
    d_pair, small, grad_project, grad_out = pl.pallas_call(
        kernel,
        out_shape=(
            jax.ShapeDtypeStruct(cells, BF16),
            jax.ShapeDtypeStruct((2, ROWS, CHANNELS), F32),
            jax.ShapeDtypeStruct((2, CHANNELS, 4 * CHANNELS), F32),
            jax.ShapeDtypeStruct((2, CHANNELS, CHANNELS), F32),
        ),
        in_specs=[whole] * 6,
        out_specs=[whole, held, whole, whole],
        scratch_shapes=scratch,
        compiler_params=pltpu.CompilerParams(
            collective_id=0, has_side_effects=True, vmem_limit_bytes=56 << 20
        ),
    )(pair_rep, cotangent, norm_gain, w_project, jnp.swapaxes(w_bias, 1, 2), w_out)
    outputs = pl.pallas_call(
        finish_kernel,
        out_shape=(
            jax.ShapeDtypeStruct(cells, BF16),
            jax.ShapeDtypeStruct((2, CHANNELS), F32),
            jax.ShapeDtypeStruct((2, CHANNELS, 4 * CHANNELS), F32),
            jax.ShapeDtypeStruct((2, HEADS, CHANNELS), F32),
            jax.ShapeDtypeStruct((2, CHANNELS, CHANNELS), F32),
        ),
        in_specs=[pl.BlockSpec(memory_space=pltpu.VMEM)] * 4,
        out_specs=[pl.BlockSpec(memory_space=pltpu.VMEM)] * 5,
    )(d_pair, small, grad_project, grad_out)
    return outputs[:3] + (jnp.swapaxes(outputs[3], 1, 2), outputs[4])


def solution(mesh):
    in_specs = (P(("dp", "dap"), None, None), P(("dp", "dap"), None, None), P(), P(), P(), P())
    out_specs = (
        P(("dp", "dap"), None, None),
        P("dp", None),
        P("dp", None, None),
        P("dp", None, None),
        P("dp", None, None),
    )
    return jax.shard_map(
        per_device, mesh=mesh, in_specs=in_specs, out_specs=out_specs, check_vma=False
    )
```
